128 devices in a mesh: dp: 16 (over x, z), tensor: 8 (over y, core).
Axes of the slice: x: 4, y: 4, z: 4, core: 2. Of those that a mesh axis runs over, the one named last changes fastest.
Arguments:
- x_seq: bfloat16 [8192, 8192], P(('dp', 'tensor')), may hold values from -0.0625 to 0.0625
- grad_out: bfloat16 [8192, 14336], P('dp', 'tensor'), may hold values from -6 to 6
- w_tiles: bfloat16 [2560, 128, 128], P('tensor'), may hold values from -0.09375 to 0.09375
- block_rows: int32 [8, 320], P('tensor'), may hold values from 0 to 63, as said below
- block_cols: int32 [8, 320], P('tensor'), may hold values from 0 to 13
- counts: int32 [8], P('tensor'), may hold values from 80 to 320, as said below
- owner: int32 [8, 320], P('tensor'), may hold values from 0 to 319, as said below
Outputs:
- grad_in: bfloat16 [8192, 8192], P(('dp', 'tensor'))
- dw_owned: float32 [8, 320, 128, 128], P('tensor', 'dp')
The draws below stay inside these ranges and needn't reach their ends.
Inputs may be any that keep to these rules, and one draw needn't show every extreme that they name: Slot k of tensor shard s keeps the block at block row block_rows[s, k] and block column block_cols[s, k]; among the first counts[s] slots of a shard no two name the same block. `counts`: some shard uses all 320 slots. `owner`: each row is a permutation of 0 to 319.
All inputs are finite; a program needn't handle non-finite values.
Results may differ from the reference program's by a relative error of at most 0.018.
Values may be sent and summed in bfloat16 or wider, within the bound.
A program may use at most 256 MiB of HBM per device.

```python
import jax
import jax.numpy as jnp
from jax import lax

D = 8192
FF = 14336
TILE = 128
KMAX = 320
SLOT_GROUP = 32
TOKENS = 8192
N_TENSOR = 8


def kept_block_positions(key):
    shard_keys = jax.random.split(jax.random.fold_in(key, 11), N_TENSOR)
    block_total = D // TILE * (FF // (TILE * N_TENSOR))
    return jax.vmap(lambda one_key: jax.random.permutation(one_key, block_total)[:KMAX])(shard_keys).astype(jnp.int32)


def draw_block_rows(key, part):
    positions = kept_block_positions(key)
    return (positions // (FF // (TILE * N_TENSOR))).astype(jnp.int32)


def draw_block_cols(key, part):
    positions = kept_block_positions(key)
    return (positions % (FF // (TILE * N_TENSOR))).astype(jnp.int32)


def draw_counts(key, part):
    key = jax.random.fold_in(key, 5)
    first_key, second_key = jax.random.split(key)
    drawn = jax.random.randint(first_key, (N_TENSOR,), KMAX // 4, KMAX + 1)
    fullest = jax.random.randint(second_key, (), 0, N_TENSOR)
    return jnp.where(jnp.arange(N_TENSOR) == fullest, KMAX, drawn).astype(jnp.int32)


def draw_owner(key, part):
    key = jax.random.fold_in(key, 7)
    shard_keys = jax.random.split(key, N_TENSOR)
    return jax.vmap(lambda one_key: jax.random.permutation(one_key, KMAX))(shard_keys).astype(jnp.int32)


def level_of(own_key, extent, shards, smallest, top_value):
    loudness = 1.0
    for dim, blocks in shards:
        steps = jax.random.uniform(jax.random.fold_in(jax.random.fold_in(own_key, 6), dim), (blocks,), jnp.float32, smallest / len(shards), top_value / len(shards))
        loudness = loudness * jnp.repeat(jnp.exp(steps), extent[dim] // blocks).reshape((-1,) + (1,) * (len(extent) - 1 - dim))
    return loudness


def normal_values(key, dims, spread, limit, cuts=(), kind=jnp.bfloat16):
    array = jax.random.normal(key, dims, jnp.float32) * spread
    if len(cuts) > 0:
        array = level_of(key, dims, cuts, -0.22, 0.18) * array
    return jnp.clip(array, min=-limit, max=limit).astype(kind)


def setup_inputs(seed: int = 0) -> dict:
    seeds = jax.random.split(jax.random.key(seed), 8)
    return {
        "x_seq": normal_values(seeds[0], (TOKENS, D), TOKENS ** -0.5, 0.0625, ((0, 128),)),
        "grad_out": normal_values(seeds[1], (TOKENS, FF), 1.0, 6.0, ((0, 16), (1, 8))),
        "w_tiles": normal_values(seeds[2], (N_TENSOR * KMAX, TILE, TILE), (FF // 4) ** -0.5, 0.09375, ((0, 8),)),
        "block_rows": draw_block_rows(jax.random.fold_in(seeds[7], 71), 0),
        "block_cols": draw_block_cols(jax.random.fold_in(seeds[7], 71), 0),
        "counts": draw_counts(jax.random.fold_in(seeds[7], 71), 0),
        "owner": draw_owner(jax.random.fold_in(seeds[7], 71), 0),
    }


def reference(x_seq, grad_out, w_tiles, block_rows, block_cols, counts, owner):
    block_count = D // TILE
    shard_cols = FF // N_TENSOR
    group_list = KMAX // SLOT_GROUP
    input_blocks_full = x_seq.reshape(TOKENS, block_count, TILE)

    def shard(running, shard_index):
        kept_rows = block_rows[shard_index]
        kept_cols = block_cols[shard_index]
        active_slot_list = jnp.arange(KMAX, dtype=jnp.int32) < counts[shard_index]
        dy_cols = lax.dynamic_slice_in_dim(grad_out, shard_index * shard_cols, shard_cols, 1)
        dy_blocks_all = dy_cols.reshape(TOKENS, shard_cols // TILE, TILE)
        tiles = lax.dynamic_slice_in_dim(w_tiles, shard_index * KMAX, KMAX, 0)

        def step(totals, group_index):
            first = group_index * SLOT_GROUP
            row_ids = lax.dynamic_slice_in_dim(kept_rows, first, SLOT_GROUP, 0)
            col_ids = lax.dynamic_slice_in_dim(kept_cols, first, SLOT_GROUP, 0)
            live_group = lax.dynamic_slice_in_dim(active_slot_list, first, SLOT_GROUP, 0)
            tile_group = lax.dynamic_slice_in_dim(tiles, first, SLOT_GROUP, 0)
            x_blocks = jnp.take(input_blocks_full, row_ids, axis=1).astype(jnp.float32)
            dy_blocks = jnp.take(dy_blocks_all, col_ids, axis=1).astype(jnp.float32)
            masked = jnp.where(live_group[:, None, None], tile_group, jnp.zeros_like(tile_group)).astype(jnp.float32)
            gradient_list = jnp.einsum("tkr,tkc->krc", x_blocks, dy_blocks)
            gradient_list = gradient_list * live_group.astype(jnp.float32)[:, None, None]
            contrib = jnp.einsum("tkc,krc->tkr", dy_blocks, masked)
            totals = totals.at[:, row_ids, :].add(contrib)
            return totals, gradient_list

        totals, gradient_list = lax.scan(step, jnp.zeros((TOKENS, block_count, TILE), jnp.float32), jnp.arange(group_list, dtype=jnp.int32))
        packed = gradient_list.reshape(KMAX, TILE, TILE)
        owned = jnp.zeros((KMAX, TILE, TILE), jnp.float32).at[owner[shard_index]].set(packed)
        part_rounded = lax.optimization_barrier(totals.reshape(TOKENS, D).astype(jnp.bfloat16))
        return running + part_rounded.astype(jnp.float32), owned

    summed, owned_all = lax.scan(shard, jnp.zeros((TOKENS, D), jnp.float32), jnp.arange(N_TENSOR, dtype=jnp.int32))
    return summed.astype(jnp.bfloat16), owned_all
```

```python
import jax
import jax.numpy as jnp
import numpy as np
from jax import lax
from jax.experimental import pallas as pl
from jax.experimental.pallas import tpu as pltpu
from jax.sharding import PartitionSpec as P

MESH = pl.DeviceIdType.MESH
RING = 4
TILE = 128
OWNERS = RING * RING
NCOPY = 64
COL_CHUNKS = 4
COL_STEP = 256
UNROLL = 4


def kernel(
    row_of, col_of, table, x_ref, g_hbm, w_hbm, gi_ref, dw_ref,
    xg, part, pr, g, gt, buf, yr1, yr2, d1, d2, d3, d4, lsem, ssem, rsem,
):
    rows, width = x_ref.shape
    tokens, shard_width = g_hbm.shape
    slots = w_hbm.shape[0]
    col_blocks = shard_width // TILE
    per_owner = slots // OWNERS
    half_own = per_owner // 2
    chunk = RING * half_own
    hrows = rows // 2
    top, bottom = pl.ds(0, hrows), pl.ds(hrows, hrows)

    p = lax.axis_index("dp")
    s = lax.axis_index("tensor")
    x, z = p // RING, p % RING
    y, q = s // 2, s % 2
    yu, yd, yo = (y + 1) % RING, (y + 3) % RING, (y + 2) % RING
    other = 1 - q

    def at_y(row, core):
        return (p, row * 2 + core)

    def at_x(pos):
        return (pos * RING + z, s)

    def at_z(pos):
        return (x * RING + pos, s)

    started = []

    def send(src, dst, device):
        i = len(started)
        copy = pltpu.make_async_remote_copy(
            src_ref=src, dst_ref=dst, send_sem=ssem.at[i], recv_sem=rsem.at[i],
            device_id=device, device_id_type=MESH,
        )
        copy.start()
        started.append(copy)
        return copy

    up, down, across = at_y(yu, q), at_y(yd, q), at_y(y, other)

    load_g = pltpu.make_async_copy(g_hbm, g, lsem.at[0])
    load_w = pltpu.make_async_copy(w_hbm, buf.at[pl.ds(0, slots)], lsem.at[1])
    load_x = pltpu.make_async_copy(x_ref, xg.at[s], lsem.at[2])
    load_g.start()
    load_w.start()
    load_x.start()

    barrier = pltpu.get_barrier_semaphore()
    peers = [
        up, down, across,
        at_x((x + 1) % RING), at_x((x + 3) % RING), at_z((z + 1) % RING), at_z((z + 3) % RING),
    ]
    for peer in peers:
        pl.semaphore_signal(barrier, inc=1, device_id=peer, device_id_type=MESH)
    pl.semaphore_wait(barrier, len(peers))

    up_top = send(x_ref.at[top], xg.at[s, top], up)
    down_bottom = send(x_ref.at[bottom], xg.at[s, bottom], down)
    up_bottom = send(x_ref.at[bottom], xg.at[s, bottom], up)
    down_top = send(x_ref.at[top], xg.at[s, top], down)
    sib_own = send(x_ref, xg.at[s], across)

    load_g.wait()
    for c in range(col_blocks):
        gt[c] = g[:, c * TILE : (c + 1) * TILE].T
    gt[col_blocks] = jnp.zeros((TILE, tokens), gt.dtype)
    buf[slots] = jnp.zeros((TILE, TILE), buf.dtype)
    load_w.wait()

    cols_per_chunk = width // COL_CHUNKS
    blocks = COL_STEP // TILE

    def part_chunk(n):
        def body(i, carry):
            first = n * cols_per_chunk + i * COL_STEP
            first_block = n * (cols_per_chunk // TILE) + i * blocks
            weight = jnp.concatenate(
                [
                    jnp.concatenate(
                        [buf[table[(first_block + b) * col_blocks + c]] for c in range(col_blocks)], axis=1
                    )
                    for b in range(blocks)
                ],
                axis=0,
            )
            product = lax.dot_general(
                g[...], weight, (((1,), (1,)), ((), ())), preferred_element_type=jnp.float32
            )
            product = product.astype(jnp.bfloat16).reshape(RING, 2, rows, COL_STEP)
            columns = pl.ds(pl.multiple_of(first, COL_STEP), COL_STEP)
            for core in range(2):
                part[core, :, :, columns] = product[:, core]
            return carry

        lax.fori_loop(0, cols_per_chunk // COL_STEP, body, 0)
        columns = pl.ds(n * cols_per_chunk, cols_per_chunk)
        return send(part.at[other, :, :, columns], pr.at[:, :, columns], across)

    pair = [part_chunk(0), part_chunk(1)]
    up_top.wait_recv()
    from_down, from_up, from_far = yd * 2 + q, yu * 2 + q, yo * 2 + q
    fwd_up = send(xg.at[from_down, top], xg.at[from_down, top], up)
    down_bottom.wait_recv()
    fwd_down = send(xg.at[from_up, bottom], xg.at[from_up, bottom], down)
    pair += [part_chunk(2), part_chunk(3)]
    up_bottom.wait_recv()
    sib_down = send(xg.at[from_down], xg.at[from_down], across)
    down_top.wait_recv()
    sib_up = send(xg.at[from_up], xg.at[from_up], across)

    for copy in pair:
        copy.wait_recv()
    row_step = 16
    steps = rows // row_step

    def add_pair(i, carry):
        at = pl.ds(pl.multiple_of((i % steps) * row_step, row_step), row_step)
        row = i // steps
        total = part[q, row, at].astype(jnp.float32) + pr[row, at].astype(jnp.float32)
        part[q, row, at] = total.astype(jnp.bfloat16)
        return carry

    lax.fori_loop(0, RING * steps, add_pair, 0)

    fwd_up.wait_recv()
    sib_far_top = send(xg.at[from_far, top], xg.at[from_far, top], across)
    fwd_down.wait_recv()
    sib_far_bottom = send(xg.at[from_far, bottom], xg.at[from_far, bottom], across)

    gi_up_far = send(part.at[q, yo, top], yr1.at[0], up)
    gi_down_far = send(part.at[q, yo, bottom], yr1.at[1], down)
    gi_up_near = send(part.at[q, yu, bottom], yr2.at[0, bottom], up)
    gi_down_near = send(part.at[q, yd, top], yr2.at[1, top], down)

    load_x.wait()
    for copy in (sib_own, sib_down, sib_up, sib_far_top, sib_far_bottom):
        copy.wait_recv()

    def tile_grads(first, count):
        def body(i, carry):
            for k in range(UNROLL):
                j = first + i * UNROLL + k
                rhs = xg[:, :, pl.ds(row_of[j] * TILE, TILE)].reshape(tokens, TILE)
                grad = jnp.dot(gt[col_of[j]], rhs, preferred_element_type=jnp.float32)
                buf[j] = grad.astype(jnp.bfloat16)
            return carry

        lax.fori_loop(0, count // UNROLL, body, 0)

    def add_tiles(dst, count, *terms):
        def body(i, carry):
            total = buf[dst + i].astype(jnp.float32)
            for ref, lead in terms:
                total = total + ref[lead + (i,)].astype(jnp.float32)
            buf[dst + i] = total.astype(jnp.bfloat16)
            return carry

        lax.fori_loop(0, count, body, 0)

    halves = [
        dict(base=0, h=0, u=x, v=z, at_u=at_x, at_v=at_z),
        dict(base=slots // 2, h=1, u=z, v=x, at_u=at_z, at_v=at_x),
    ]
    hc = chunk // 2
    for f in halves:
        h, u, at_u = f["h"], f["u"], f["at_u"]
        f["uu"], f["ud"] = (u + 1) % RING, (u + 3) % RING
        f["far"] = f["base"] + ((u + 2) % RING) * chunk
        f["next"] = f["base"] + f["uu"] * chunk
        f["prev"] = f["base"] + f["ud"] * chunk
        f["own"] = f["base"] + u * chunk
        tile_grads(f["far"], hc)
        f["s1u"] = send(buf.at[pl.ds(f["far"], hc)], d1.at[h, 0], at_u(f["uu"]))
        tile_grads(f["far"] + hc, hc)
        f["s1d"] = send(buf.at[pl.ds(f["far"] + hc, hc)], d1.at[h, 1], at_u(f["ud"]))
    for f in halves:
        h, at_u = f["h"], f["at_u"]
        tile_grads(f["next"] + hc, hc)
        f["s2un"] = send(buf.at[pl.ds(f["next"] + hc, hc)], d2.at[h, 0, pl.ds(hc, hc)], at_u(f["uu"]))
        tile_grads(f["prev"], hc)
        f["s2dn"] = send(buf.at[pl.ds(f["prev"], hc)], d2.at[h, 1, pl.ds(0, hc)], at_u(f["ud"]))
    for f in halves:
        tile_grads(f["next"], hc)
        tile_grads(f["prev"] + hc, hc)
    for f in halves:
        h, at_u = f["h"], f["at_u"]
        f["s1u"].wait_recv()
        add_tiles(f["next"], hc, (d1, (h, 0)))
        f["s2uf"] = send(buf.at[pl.ds(f["next"], hc)], d2.at[h, 0, pl.ds(0, hc)], at_u(f["uu"]))
        f["s1d"].wait_recv()
        add_tiles(f["prev"] + hc, hc, (d1, (h, 1)))
        f["s2df"] = send(buf.at[pl.ds(f["prev"] + hc, hc)], d2.at[h, 1, pl.ds(hc, hc)], at_u(f["ud"]))
    for f in halves:
        tile_grads(f["own"], chunk)

    def add_rows(row, first, term):
        def body(i, carry):
            at = pl.ds(pl.multiple_of(i * row_step, row_step), row_step)
            to = pl.ds(pl.multiple_of(first + i * row_step, row_step), row_step)
            total = part[q, row, to].astype(jnp.float32) + yr1[term, at].astype(jnp.float32)
            part[q, row, to] = total.astype(jnp.bfloat16)
            return carry

        lax.fori_loop(0, hrows // row_step, body, 0)

    gi_up_far.wait_recv()
    add_rows(yu, 0, 0)
    gi_up_sum = send(part.at[q, yu, top], yr2.at[0, top], up)
    gi_down_far.wait_recv()
    add_rows(yd, hrows, 1)
    gi_down_sum = send(part.at[q, yd, bottom], yr2.at[1, bottom], down)

    qc = half_own // 2
    for f in halves:
        h, v, at_v = f["h"], f["v"], f["at_v"]
        for name in ("s2un", "s2dn", "s2uf", "s2df"):
            f[name].wait_recv()
        vu, vd, vo = (v + 1) % RING, (v + 3) % RING, (v + 2) % RING
        f["vu"], f["vd"] = vu, vd

        def settle(pos, f=f, h=h):
            lead = pos * half_own

            def body(i, carry):
                total = buf[f["own"] + lead + i].astype(jnp.float32)
                total = total + d2[h, 0, lead + i].astype(jnp.float32)
                total = total + d2[h, 1, lead + i].astype(jnp.float32)
                buf[f["own"] + lead + i] = total.astype(jnp.bfloat16)
                return carry

            lax.fori_loop(0, half_own, body, 0)
            return f["own"] + lead

        far = settle(vo)
        f["t1u"] = send(buf.at[pl.ds(far, qc)], d3.at[h, 0], at_v(vu))
        f["t1d"] = send(buf.at[pl.ds(far + qc, qc)], d3.at[h, 1], at_v(vd))
        f["n2"] = settle(vu)
        f["t2un"] = send(buf.at[pl.ds(f["n2"] + qc, qc)], d4.at[h, 0, pl.ds(qc, qc)], at_v(vu))
        f["p2"] = settle(vd)
        f["t2dn"] = send(buf.at[pl.ds(f["p2"], qc)], d4.at[h, 1, pl.ds(0, qc)], at_v(vd))
        f["o2"] = settle(v)
    for f in halves:
        h, at_v = f["h"], f["at_v"]
        f["t1u"].wait_recv()
        add_tiles(f["n2"], qc, (d3, (h, 0)))
        f["t2uf"] = send(buf.at[pl.ds(f["n2"], qc)], d4.at[h, 0, pl.ds(0, qc)], at_v(f["vu"]))
        f["t1d"].wait_recv()
        add_tiles(f["p2"] + qc, qc, (d3, (h, 1)))
        f["t2df"] = send(buf.at[pl.ds(f["p2"] + qc, qc)], d4.at[h, 1, pl.ds(qc, qc)], at_v(f["vd"]))

    for copy in (gi_up_near, gi_down_near, gi_up_sum, gi_down_sum):
        copy.wait_recv()

    def finish_rows(i, carry):
        at = pl.ds(pl.multiple_of(i * row_step, row_step), row_step)
        total = part[q, y, at].astype(jnp.float32) + yr2[0, at].astype(jnp.float32)
        gi_ref[at, :] = (total + yr2[1, at].astype(jnp.float32)).astype(jnp.bfloat16)
        return carry

    lax.fori_loop(0, steps, finish_rows, 0)

    for f in halves:
        h = f["h"]
        for name in ("t2un", "t2dn", "t2uf", "t2df"):
            f[name].wait_recv()

        def finish_tiles(i, carry, f=f, h=h):
            total = buf[f["o2"] + i].astype(jnp.float32) + d4[h, 0, i].astype(jnp.float32)
            total = total + d4[h, 1, i].astype(jnp.float32)
            dw_ref[h * half_own + i] = total.T
            return carry

        lax.fori_loop(0, half_own, finish_tiles, 0)
    for copy in started:
        copy.wait_send()


def per_device(x_seq, grad_out, w_tiles, block_rows, block_cols, counts, owner):
    rows, width = x_seq.shape
    tokens, shard_width = grad_out.shape
    slots = w_tiles.shape[0]
    col_blocks = shard_width // TILE
    per_owner = slots // OWNERS
    half_own = per_owner // 2
    slot = jnp.arange(slots, dtype=jnp.int32)
    live = slot < counts[0]

    ids = np.arange(slots, dtype=np.int32).reshape(RING, RING, 2, half_own)
    places = np.concatenate([ids[:, :, 0].reshape(-1), ids[:, :, 1].transpose(1, 0, 2).reshape(-1)])
    code = block_rows[0] * 16 + jnp.where(live, block_cols[0], col_blocks)
    codes = jnp.sum(jnp.where(owner[0][None, :] == places[:, None], code[None, :], 0), axis=1)
    row_of, col_of = codes // 16, codes % 16
    key = jnp.where(live, block_rows[0] * col_blocks + block_cols[0], -1)
    block = jnp.arange(width // TILE * col_blocks, dtype=jnp.int32)
    table = slots + jnp.sum(jnp.where(key[None, :] == block[:, None], slot[None, :] - slots, 0), axis=1)

    bf16 = jnp.bfloat16
    chunk = RING * half_own
    any_space = pl.BlockSpec(memory_space=pl.ANY)
    smem = pl.BlockSpec(memory_space=pltpu.SMEM)
    vmem = pl.BlockSpec(memory_space=pltpu.VMEM)
    grad_in, owned = pl.pallas_call(
        kernel,
        out_shape=(
            jax.ShapeDtypeStruct((rows, width), bf16),
            jax.ShapeDtypeStruct((per_owner, TILE, TILE), jnp.float32),
        ),
        in_specs=[smem, smem, smem, any_space, any_space, any_space],
        out_specs=(vmem, vmem),
        scratch_shapes=[
            pltpu.VMEM((2 * RING, rows, width), bf16),
            pltpu.VMEM((2, RING, rows, width), bf16),
            pltpu.VMEM((RING, rows, width), bf16),
            pltpu.VMEM((tokens, shard_width), bf16),
            pltpu.VMEM((col_blocks + 1, TILE, tokens), bf16),
            pltpu.VMEM((slots + 1, TILE, TILE), bf16),
            pltpu.VMEM((2, rows // 2, width), bf16),
            pltpu.VMEM((2, rows, width), bf16),
            pltpu.VMEM((2, 2, chunk // 2, TILE, TILE), bf16),
            pltpu.VMEM((2, 2, chunk, TILE, TILE), bf16),
            pltpu.VMEM((2, 2, half_own // 2, TILE, TILE), bf16),
            pltpu.VMEM((2, 2, half_own, TILE, TILE), bf16),
            pltpu.SemaphoreType.DMA((3,)),
            pltpu.SemaphoreType.DMA((NCOPY,)),
            pltpu.SemaphoreType.DMA((NCOPY,)),
        ],
        compiler_params=pltpu.CompilerParams(
            collective_id=0, has_side_effects=True, vmem_limit_bytes=60 * 1024 * 1024
        ),
        cost_estimate=pl.CostEstimate(
            flops=2 * tokens * shard_width * width + 2 * slots * tokens * TILE * TILE,
            bytes_accessed=2 * (slots * TILE * TILE + tokens * shard_width + 2 * rows * width)
            + 4 * per_owner * TILE * TILE,
            transcendentals=0,
        ),
    )(row_of, col_of, table, x_seq, grad_out, w_tiles)
    return grad_in, owned.reshape(1, per_owner, TILE, TILE)


def solution(mesh):
    return jax.shard_map(
        per_device,
        mesh=mesh,
        in_specs=(
            P(("dp", "tensor"), None),
            P("dp", "tensor"),
            P("tensor", None, None),
            P("tensor", None),
            P("tensor", None),
            P("tensor"),
            P("tensor", None),
        ),
        out_specs=(P(("dp", "tensor"), None), P("tensor", "dp", None, None)),
        check_vma=False,
    )
```

```python
import jax
import jax.numpy as jnp
import numpy as np
from jax import lax
from jax.experimental import pallas as pl
from jax.experimental.pallas import tpu as pltpu
from jax.sharding import PartitionSpec as P

MESH = pl.DeviceIdType.MESH
RING = 4
TILE = 128
OWNERS = RING * RING
NCOPY = 80
COL_CHUNKS = 4
COL_STEP = 256
UNROLL = 5


def kernel(
    lut, x_ref, g_hbm, w_hbm, gi_ref, dw_ref,
    xg, part, pr, g, gt, buf, yr1, yr2, d1, d2, d3, d4, lsem, ssem, rsem,
):
    rows, width = x_ref.shape
    tokens, shard_width = g_hbm.shape
    slots = w_hbm.shape[0]
    col_blocks = shard_width // TILE
    per_owner = slots // OWNERS
    group = per_owner // 4
    chunk = RING * group
    piece = RING * chunk
    hc = chunk // 2
    hrows = rows // 2
    top, bottom = pl.ds(0, hrows), pl.ds(hrows, hrows)

    p = lax.axis_index("dp")
    s = lax.axis_index("tensor")
    x, z = p // RING, p % RING
    y, q = s // 2, s % 2
    yu, yd, yo = (y + 1) % RING, (y + 3) % RING, (y + 2) % RING
    other = 1 - q

    def at_y(row, core):
        return (p, row * 2 + core)

    def at_x(pos):
        return (pos * RING + z, s)

    def at_z(pos):
        return (x * RING + pos, s)

    started = []

    def send(src, dst, device):
        i = len(started)
        copy = pltpu.make_async_remote_copy(
            src_ref=src, dst_ref=dst, send_sem=ssem.at[i], recv_sem=rsem.at[i],
            device_id=device, device_id_type=MESH,
        )
        copy.start()
        started.append(copy)
        return copy

    up, down, across = at_y(yu, q), at_y(yd, q), at_y(y, other)

    load_x = pltpu.make_async_copy(x_ref, xg.at[s], lsem.at[0])
    load_g = pltpu.make_async_copy(g_hbm, g, lsem.at[1])
    load_w = pltpu.make_async_copy(w_hbm, buf.at[pl.ds(0, slots)], lsem.at[2])
    load_x.start()

    barrier = pltpu.get_barrier_semaphore()
    peers = [
        up, down, across,
        at_x((x + 1) % RING), at_x((x + 3) % RING), at_z((z + 1) % RING), at_z((z + 3) % RING),
    ]
    for peer in peers:
        pl.semaphore_signal(barrier, inc=1, device_id=peer, device_id_type=MESH)
    load_x.wait()
    pl.semaphore_wait(barrier, len(peers))

    up_top = send(xg.at[s, top], xg.at[s, top], up)
    down_bottom = send(xg.at[s, bottom], xg.at[s, bottom], down)
    up_bottom = send(xg.at[s, bottom], xg.at[s, bottom], up)
    down_top = send(xg.at[s, top], xg.at[s, top], down)
    sib_own = send(xg.at[s], xg.at[s], across)

    load_g.start()
    load_w.start()
    load_g.wait()
    for c in range(col_blocks):
        gt[c] = g[:, c * TILE : (c + 1) * TILE].T
    gt[col_blocks] = jnp.zeros((TILE, tokens), gt.dtype)
    buf[slots] = jnp.zeros((TILE, TILE), buf.dtype)
    load_w.wait()

    cols_per_chunk = width // COL_CHUNKS
    blocks = COL_STEP // TILE

    def part_chunk(n):
        def body(i, carry):
            first = n * cols_per_chunk + i * COL_STEP
            first_block = n * (cols_per_chunk // TILE) + i * blocks
            weight = jnp.concatenate(
                [
                    jnp.concatenate(
                        [buf[lut[slots + (first_block + b) * col_blocks + c] + slots] for c in range(col_blocks)], axis=1
                    )
                    for b in range(blocks)
                ],
                axis=0,
            )
            product = lax.dot_general(
                g[...], weight, (((1,), (1,)), ((), ())), preferred_element_type=jnp.float32
            )
            product = product.astype(jnp.bfloat16).reshape(RING, 2, rows, COL_STEP)
            columns = pl.ds(pl.multiple_of(first, COL_STEP), COL_STEP)
            for core in range(2):
                part[core, :, :, columns] = product[:, core]
            return carry

        lax.fori_loop(0, cols_per_chunk // COL_STEP, body, 0)
        columns = pl.ds(n * cols_per_chunk, cols_per_chunk)
        return send(part.at[other, :, :, columns], pr.at[:, :, columns], across)

    pair = [part_chunk(0), part_chunk(1)]
    up_top.wait_recv()
    from_down, from_up, from_far = yd * 2 + q, yu * 2 + q, yo * 2 + q
    fwd_up = send(xg.at[from_down, top], xg.at[from_down, top], up)
    down_bottom.wait_recv()
    fwd_down = send(xg.at[from_up, bottom], xg.at[from_up, bottom], down)
    pair += [part_chunk(2), part_chunk(3)]
    up_bottom.wait_recv()
    sib_down = send(xg.at[from_down], xg.at[from_down], across)
    down_top.wait_recv()
    sib_up = send(xg.at[from_up], xg.at[from_up], across)

    for copy in pair:
        copy.wait_recv()
    row_step = 16
    steps = rows // row_step

    def add_pair(i, carry):
        at = pl.ds(pl.multiple_of((i % steps) * row_step, row_step), row_step)
        row = i // steps
        total = part[q, row, at].astype(jnp.float32) + pr[row, at].astype(jnp.float32)
        part[q, row, at] = total.astype(jnp.bfloat16)
        return carry

    lax.fori_loop(0, RING * steps, add_pair, 0)

    fwd_up.wait_recv()
    sib_far_top = send(xg.at[from_far, top], xg.at[from_far, top], across)
    fwd_down.wait_recv()
    sib_far_bottom = send(xg.at[from_far, bottom], xg.at[from_far, bottom], across)

    gi_up_far = send(part.at[q, yo, top], yr1.at[0], up)
    gi_down_far = send(part.at[q, yo, bottom], yr1.at[1], down)
    gi_up_near = send(part.at[q, yu, bottom], yr2.at[0, bottom], up)
    gi_down_near = send(part.at[q, yd, top], yr2.at[1, top], down)

    for copy in (sib_own, sib_down, sib_up, sib_far_top, sib_far_bottom):
        copy.wait_recv()

    def tile_grads(first, count):
        def body(i, carry):
            for k in range(UNROLL):
                j = first + i * UNROLL + k
                code = lut[j]
                rhs = xg[:, :, pl.ds(lax.div(code, 16) * TILE, TILE)].reshape(tokens, TILE)
                grad = jnp.dot(gt[lax.rem(code, 16)], rhs, preferred_element_type=jnp.float32)
                buf[j] = grad.astype(jnp.bfloat16)
            return carry

        lax.fori_loop(0, count // UNROLL, body, 0)

    def piece_of(h, i):
        u, v, at_u, at_v = (x, z, at_x, at_z) if h == 0 else (z, x, at_z, at_x)
        n = h * 2 + i
        first = n * piece
        uu, ud, uo = (u + 1) % RING, (u + 3) % RING, (u + 2) % RING
        return dict(
            n=n, v=v, to_uu=at_u(uu), to_ud=at_u(ud), vu=(v + 1) % RING, vd=(v + 3) % RING,
            vo=(v + 2) % RING, at_v=at_v, far=first + uo * chunk, next=first + uu * chunk,
            prev=first + ud * chunk, own=first + u * chunk,
        )

    low, high = pl.ds(0, TILE // 2), pl.ds(TILE // 2, TILE // 2)

    def some(first, count):
        return buf.at[pl.ds(first, count)]

    def far_out(f):
        n = f["n"]
        tile_grads(f["far"], hc)
        f["far_u"] = send(some(f["far"], hc), d1.at[n, 0], f["to_uu"])
        tile_grads(f["far"] + hc, hc)
        f["far_d"] = send(some(f["far"] + hc, hc), d1.at[n, 1], f["to_ud"])

    def near_out(f):
        n = f["n"]
        tile_grads(f["next"] + hc, hc)
        f["near_u"] = send(some(f["next"] + hc, hc), d2.at[n, 0, pl.ds(hc, hc)], f["to_uu"])
        tile_grads(f["prev"], hc)
        f["near_d"] = send(some(f["prev"], hc), d2.at[n, 1, pl.ds(0, hc)], f["to_ud"])

    def near_rest(f):
        tile_grads(f["next"], hc)
        tile_grads(f["prev"] + hc, hc)

    def add_far(f, dst, side):
        def body(i, carry):
            total = buf[dst + i].astype(jnp.float32) + d1[f["n"], side, i].astype(jnp.float32)
            buf[dst + i] = total.astype(jnp.bfloat16)
            return carry

        lax.fori_loop(0, hc, body, 0)

    def sums_out(f):
        n = f["n"]
        f["far_u"].wait_recv()
        add_far(f, f["next"], 0)
        f["sum_u"] = send(some(f["next"], hc), d2.at[n, 0, pl.ds(0, hc)], f["to_uu"])
        f["far_d"].wait_recv()
        add_far(f, f["prev"] + hc, 1)
        f["sum_d"] = send(some(f["prev"] + hc, hc), d2.at[n, 1, pl.ds(hc, hc)], f["to_ud"])

    def settle(f, pos):
        n, lead = f["n"], pos * group

        def body(i, carry):
            total = buf[f["own"] + lead + i].astype(jnp.float32)
            total = total + d2[n, 0, lead + i].astype(jnp.float32)
            total = total + d2[n, 1, lead + i].astype(jnp.float32)
            buf[f["own"] + lead + i] = total.astype(jnp.bfloat16)
            return carry

        lax.fori_loop(0, group, body, 0)
        return pl.ds(f["own"] + lead, group)

    def second_out(f):
        n, to_vu, to_vd = f["n"], f["at_v"](f["vu"]), f["at_v"](f["vd"])
        for name in ("near_u", "near_d", "sum_u", "sum_d"):
            f[name].wait_recv()
        far = settle(f, f["vo"])
        f["far_u2"] = send(buf.at[far, low], d3.at[n, 0], to_vu)
        f["far_d2"] = send(buf.at[far, high], d3.at[n, 1], to_vd)
        following = settle(f, f["vu"])
        f["near_u2"] = send(buf.at[following, high], d4.at[n, 0, :, high], to_vu)
        preceding = settle(f, f["vd"])
        f["near_d2"] = send(buf.at[preceding, low], d4.at[n, 1, :, low], to_vd)
        settle(f, f["v"])

    def second_sums(f):
        n, to_vu, to_vd = f["n"], f["at_v"](f["vu"]), f["at_v"](f["vd"])
        for name, side, pos, half, dev in (("u", 0, "vu", low, to_vu), ("d", 1, "vd", high, to_vd)):
            f[f"far_{name}2"].wait_recv()
            dst = f["own"] + f[pos] * group

            def body(i, carry, dst=dst, half=half, side=side):
                total = buf[dst + i, half].astype(jnp.float32) + d3[n, side, i].astype(jnp.float32)
                buf[dst + i, half] = total.astype(jnp.bfloat16)
                return carry

            lax.fori_loop(0, group, body, 0)
            f[f"sum_{name}2"] = send(buf.at[pl.ds(dst, group), half], d4.at[n, side, :, half], dev)

    def finish(f):
        n = f["n"]
        for name in ("near_u2", "near_d2", "sum_u2", "sum_d2"):
            f[name].wait_recv()

        def body(i, carry):
            total = buf[f["own"] + f["v"] * group + i].astype(jnp.float32)
            total = total + d4[n, 0, i].astype(jnp.float32) + d4[n, 1, i].astype(jnp.float32)
            dw_ref[n * group + i] = total.T
            return carry

        lax.fori_loop(0, group, body, 0)

    def add_rows(row, first, term):
        def body(i, carry):
            at = pl.ds(pl.multiple_of(i * row_step, row_step), row_step)
            to = pl.ds(pl.multiple_of(first + i * row_step, row_step), row_step)
            total = part[q, row, to].astype(jnp.float32) + yr1[term, at].astype(jnp.float32)
            part[q, row, to] = total.astype(jnp.bfloat16)
            return carry

        lax.fori_loop(0, hrows // row_step, body, 0)

    early = [piece_of(0, 0), piece_of(1, 0)]
    late = [piece_of(0, 1), piece_of(1, 1)]
    for f in early:
        far_out(f)
    for f in early:
        near_out(f)
    for f in early:
        near_rest(f)
    for f in late:
        far_out(f)
    for f in early:
        sums_out(f)
    for f in late:
        near_out(f)
    for f in late:
        near_rest(f)
    for f in early + late:
        tile_grads(f["own"], chunk)
    for f in late:
        sums_out(f)

    gi_up_far.wait_recv()
    add_rows(yu, 0, 0)
    gi_up_sum = send(part.at[q, yu, top], yr2.at[0, top], up)
    gi_down_far.wait_recv()
    add_rows(yd, hrows, 1)
    gi_down_sum = send(part.at[q, yd, bottom], yr2.at[1, bottom], down)

    for f in early:
        second_out(f)
    for f in early:
        second_sums(f)
    for f in late:
        second_out(f)
    for f in late:
        second_sums(f)

    for copy in (gi_up_near, gi_down_near, gi_up_sum, gi_down_sum):
        copy.wait_recv()

    def finish_rows(i, carry):
        at = pl.ds(pl.multiple_of(i * row_step, row_step), row_step)
        total = part[q, y, at].astype(jnp.float32) + yr2[0, at].astype(jnp.float32)
        gi_ref[at, :] = (total + yr2[1, at].astype(jnp.float32)).astype(jnp.bfloat16)
        return carry

    lax.fori_loop(0, steps, finish_rows, 0)
    for f in early + late:
        finish(f)
    for copy in started:
        copy.wait_send()


def per_device(x_seq, grad_out, w_tiles, block_rows, block_cols, counts, owner):
    rows, width = x_seq.shape
    tokens, shard_width = grad_out.shape
    slots = w_tiles.shape[0]
    col_blocks = shard_width // TILE
    per_owner = slots // OWNERS
    group = per_owner // 4
    chunk = RING * group
    slot = jnp.arange(slots, dtype=jnp.int32)[None, :]
    live = slot < counts[0]

    ids = np.arange(slots, dtype=np.int32).reshape(RING, RING, 2, 2 * group)
    ids = np.stack([ids[:, :, 0], ids[:, :, 1].transpose(1, 0, 2)]).reshape(2, RING, RING, 2, group)
    places = ids.transpose(0, 3, 1, 2, 4).reshape(-1)
    code = block_rows * 16 + jnp.where(live, block_cols, col_blocks)
    key = jnp.where(live, block_rows * col_blocks + block_cols, -1)
    blocks = width // TILE * col_blocks
    wanted = np.concatenate([places, np.arange(blocks, dtype=np.int32)])[:, None]
    is_place = np.arange(slots + blocks)[:, None] < slots
    match = jnp.where(is_place, owner, key) == wanted
    lut = jnp.sum(jnp.where(match, jnp.where(is_place, code, slot - slots), 0), axis=1)

    bf16 = jnp.bfloat16
    any_space = pl.BlockSpec(memory_space=pl.ANY)
    smem = pl.BlockSpec(memory_space=pltpu.SMEM)
    vmem = pl.BlockSpec(memory_space=pltpu.VMEM)
    grad_in, owned = pl.pallas_call(
        kernel,
        out_shape=(
            jax.ShapeDtypeStruct((rows, width), bf16),
            jax.ShapeDtypeStruct((per_owner, TILE, TILE), jnp.float32),
        ),
        in_specs=[smem, any_space, any_space, any_space],
        out_specs=(vmem, vmem),
        scratch_shapes=[
            pltpu.VMEM((2 * RING, rows, width), bf16),
            pltpu.VMEM((2, RING, rows, width), bf16),
            pltpu.VMEM((RING, rows, width), bf16),
            pltpu.VMEM((tokens, shard_width), bf16),
            pltpu.VMEM((col_blocks + 1, TILE, tokens), bf16),
            pltpu.VMEM((slots + 1, TILE, TILE), bf16),
            pltpu.VMEM((2, rows // 2, width), bf16),
            pltpu.VMEM((2, rows, width), bf16),
            pltpu.VMEM((4, 2, chunk // 2, TILE, TILE), bf16),
            pltpu.VMEM((4, 2, chunk, TILE, TILE), bf16),
            pltpu.VMEM((4, 2, group, TILE // 2, TILE), bf16),
            pltpu.VMEM((4, 2, group, TILE, TILE), bf16),
            pltpu.SemaphoreType.DMA((3,)),
            pltpu.SemaphoreType.DMA((NCOPY,)),
            pltpu.SemaphoreType.DMA((NCOPY,)),
        ],
        compiler_params=pltpu.CompilerParams(
            collective_id=0, has_side_effects=True, vmem_limit_bytes=60 * 1024 * 1024
        ),
        cost_estimate=pl.CostEstimate(
            flops=2 * tokens * shard_width * width + 2 * slots * tokens * TILE * TILE,
            bytes_accessed=2 * (slots * TILE * TILE + tokens * shard_width + 2 * rows * width)
            + 4 * per_owner * TILE * TILE,
            transcendentals=0,
        ),
    )(lut, x_seq, grad_out, w_tiles)
    return grad_in, owned.reshape(1, per_owner, TILE, TILE)


def solution(mesh):
    return jax.shard_map(
        per_device,
        mesh=mesh,
        in_specs=(
            P(("dp", "tensor"), None),
            P("dp", "tensor"),
            P("tensor", None, None),
            P("tensor", None),
            P("tensor", None),
            P("tensor"),
            P("tensor", None),
        ),
        out_specs=(P(("dp", "tensor"), None), P("tensor", "dp", None, None)),
        check_vma=False,
    )
```

```python
import jax
import jax.numpy as jnp
from jax import lax
from jax.experimental import pallas as pl
from jax.experimental.pallas import tpu as pltpu
from jax.sharding import PartitionSpec as P

MESH = pl.DeviceIdType.MESH
RING = 4
TILE = 128
OWNERS = RING * RING
NCOPY = 80
COL_CHUNKS = 4
COL_STEP = 256
UNROLL = 4


def pieces_of(per_owner):
    half = per_owner // 2
    late = half * 2 // 5
    return (half - late, late)


def fill_tables(rows_ref, cols_ref, owner_ref, counts, lut_v, col_blocks, blocks):
    slots = owner_ref.shape[1]
    per_owner = slots // OWNERS
    half = per_owner // 2
    early, late = pieces_of(per_owner)
    slot = lax.broadcasted_iota(jnp.int32, (1, slots), 1)
    live = (slot < counts[0]).astype(jnp.int32)

    def quotient(a, n, limit):
        return sum((a >= n * m).astype(jnp.int32) for m in range(1, limit))

    at = owner_ref[...]
    chip = quotient(at, per_owner, OWNERS)
    at = at - chip * per_owner
    x = quotient(chip, RING, RING)
    z = chip - x * RING
    h = (at >= half).astype(jnp.int32)
    at = at - h * half
    i = (at >= early).astype(jnp.int32)
    at = at - i * early
    u, v = x + h * (z - x), z + h * (x - z)
    place = (h * half + i * early) * OWNERS + (u * RING + v) * (early + i * (late - early)) + at
    code = rows_ref[...] * 16 + col_blocks + live * (cols_ref[...] - col_blocks)
    key = live * (rows_ref[...] * col_blocks + cols_ref[...] + 1) - 1

    places, tables = pl.cdiv(slots, TILE), pl.cdiv(blocks, TILE)
    totals = [jnp.zeros((1, TILE), jnp.int32) for _ in range(places + tables)]
    for first in range(0, slots, TILE):
        n = min(TILE, slots - first)

        def upright(a, first=first, n=n):
            return jnp.broadcast_to(a[:, first : first + n], (TILE, n)).T

        lane = lax.broadcasted_iota(jnp.int32, (n, TILE), 1)
        index = lax.broadcasted_iota(jnp.int32, (n, TILE), 0) + (first - slots)
        place_n, code_n, key_n = upright(place), upright(code), upright(key)
        for m in range(places + tables):
            wanted, had, value = (
                (lane + m * TILE, place_n, code_n) if m < places else (lane + (m - places) * TILE, key_n, index)
            )
            match = (had == wanted).astype(jnp.int32)
            if m < places:
                totals[m] = jnp.maximum(totals[m], jnp.max(match * value, axis=0, keepdims=True))
            else:
                totals[m] = jnp.minimum(totals[m], jnp.min(match * value, axis=0, keepdims=True))
    lut_v[...] = jnp.zeros_like(lut_v)
    for m, total in enumerate(totals):
        lut_v[m : m + 1, :] = total


def kernel(
    rows_ref, cols_ref, owner_ref, counts, x_ref, g_hbm, w_hbm, gi_ref, dw_ref,
    xg, part, pr, g, gt, buf, yr1, yr2, e1, e2, e3, e4, l1, l2, l3, l4, lut_v, lut_s, lsem, ssem, rsem,
):
    rows, width = x_ref.shape
    tokens, shard_width = g_hbm.shape
    slots = w_hbm.shape[0]
    col_blocks = shard_width // TILE
    per_owner = slots // OWNERS
    hrows = rows // 2
    top, bottom = pl.ds(0, hrows), pl.ds(hrows, hrows)
    quarters = [pl.ds(i * (rows // 4), rows // 4) for i in range(4)]

    p = lax.axis_index("dp")
    s = lax.axis_index("tensor")
    x, z = p // RING, p % RING
    y, q = s // 2, s % 2
    yu, yd, yo = (y + 1) % RING, (y + 3) % RING, (y + 2) % RING
    other = 1 - q

    def at_y(row, core):
        return (p, row * 2 + core)

    def at_x(pos):
        return (pos * RING + z, s)

    def at_z(pos):
        return (x * RING + pos, s)

    started = []

    def send(src, dst, device):
        i = len(started)
        copy = pltpu.make_async_remote_copy(
            src_ref=src, dst_ref=dst, send_sem=ssem.at[i], recv_sem=rsem.at[i],
            device_id=device, device_id_type=MESH,
        )
        copy.start()
        started.append(copy)
        return copy

    left = []

    def sent(copy):
        copy.wait_send()
        left.append(copy)

    up, down, across = at_y(yu, q), at_y(yd, q), at_y(y, other)

    load_x = pltpu.make_async_copy(x_ref, xg.at[s], lsem.at[0])
    load_g = pltpu.make_async_copy(g_hbm, g, lsem.at[1])
    load_w = pltpu.make_async_copy(w_hbm, buf.at[pl.ds(0, slots)], lsem.at[2])
    load_x.start()

    barrier = pltpu.get_barrier_semaphore()
    peers = [
        up, down, across,
        at_x((x + 1) % RING), at_x((x + 3) % RING), at_z((z + 1) % RING), at_z((z + 3) % RING),
    ]
    for peer in peers:
        pl.semaphore_signal(barrier, inc=1, device_id=peer, device_id_type=MESH)
    load_x.wait()
    pl.semaphore_wait(barrier, len(peers))

    up_top = send(xg.at[s, top], xg.at[s, top], up)
    down_bottom = send(xg.at[s, bottom], xg.at[s, bottom], down)
    up_bottom = send(xg.at[s, bottom], xg.at[s, bottom], up)
    down_top = send(xg.at[s, top], xg.at[s, top], down)
    sib_own = send(xg.at[s], xg.at[s], across)

    load_g.start()
    load_w.start()
    fill_tables(rows_ref, cols_ref, owner_ref, counts, lut_v, col_blocks, width // TILE * col_blocks)
    load_lut = pltpu.make_async_copy(lut_v, lut_s, lsem.at[3])
    load_lut.start()
    load_g.wait()
    for c in range(col_blocks):
        gt[c] = g[:, c * TILE : (c + 1) * TILE].T
    gt[col_blocks] = jnp.zeros((TILE, tokens), gt.dtype)
    buf[slots] = jnp.zeros((TILE, TILE), buf.dtype)
    load_w.wait()
    load_lut.wait()

    table_at = pl.cdiv(slots, TILE) * TILE

    def lut(i):
        return lut_s[lax.div(i, TILE), lax.rem(i, TILE)]

    cols_per_chunk = width // COL_CHUNKS
    blocks = COL_STEP // TILE

    def part_chunk(n):
        def body(i, carry):
            first = n * cols_per_chunk + i * COL_STEP
            first_block = n * (cols_per_chunk // TILE) + i * blocks
            weight = jnp.concatenate(
                [
                    jnp.concatenate(
                        [buf[lut(table_at + (first_block + b) * col_blocks + c) + slots] for c in range(col_blocks)], axis=1
                    )
                    for b in range(blocks)
                ],
                axis=0,
            )
            product = lax.dot_general(
                g[...], weight, (((1,), (1,)), ((), ())), preferred_element_type=jnp.float32
            )
            product = product.astype(jnp.bfloat16).reshape(RING, 2, rows, COL_STEP)
            columns = pl.ds(pl.multiple_of(first, COL_STEP), COL_STEP)
            for core in range(2):
                part[core, :, :, columns] = product[:, core]
            return carry

        lax.fori_loop(0, cols_per_chunk // COL_STEP, body, 0)
        columns = pl.ds(n * cols_per_chunk, cols_per_chunk)
        return send(part.at[other, :, :, columns], pr.at[:, :, columns], across)

    pair = [part_chunk(0), part_chunk(1)]
    up_top.wait_recv()
    from_down, from_up, from_far = yd * 2 + q, yu * 2 + q, yo * 2 + q
    fwd_up = [send(xg.at[from_down, at], xg.at[from_down, at], up) for at in quarters[:2]]
    down_bottom.wait_recv()
    fwd_down = [send(xg.at[from_up, at], xg.at[from_up, at], down) for at in quarters[2:]]
    pair += [part_chunk(2), part_chunk(3)]
    up_bottom.wait_recv()
    sib_down = send(xg.at[from_down], xg.at[from_down], across)
    down_top.wait_recv()
    sib_up = send(xg.at[from_up], xg.at[from_up], across)

    for copy in pair:
        copy.wait_recv()
    row_step = 16
    steps = rows // row_step

    def add_pair(i, carry):
        at = pl.ds(pl.multiple_of((i % steps) * row_step, row_step), row_step)
        row = i // steps
        total = part[q, row, at].astype(jnp.float32) + pr[row, at].astype(jnp.float32)
        part[q, row, at] = total.astype(jnp.bfloat16)
        return carry

    lax.fori_loop(0, RING * steps, add_pair, 0)

    sib_far = []
    for i in range(2):
        for copy, at in ((fwd_up[i], quarters[i]), (fwd_down[i], quarters[i + 2])):
            copy.wait_recv()
            sib_far.append(send(xg.at[from_far, at], xg.at[from_far, at], across))

    gi_up_far = send(part.at[q, yo, top], yr1.at[0], up)
    gi_down_far = send(part.at[q, yo, bottom], yr1.at[1], down)
    gi_up_near = send(part.at[q, yu, bottom], yr2.at[0, bottom], up)
    gi_down_near = send(part.at[q, yd, top], yr2.at[1, top], down)

    for copy in (sib_own, sib_down, sib_up, *sib_far):
        copy.wait_recv()

    def tile_grads(first, count):
        def body(i, carry):
            for k in range(UNROLL):
                j = first + i * UNROLL + k
                code = lut(j)
                rhs = xg[:, :, pl.ds(lax.div(code, 16) * TILE, TILE)].reshape(tokens, TILE)
                grad = jnp.dot(gt[lax.rem(code, 16)], rhs, preferred_element_type=jnp.float32)
                buf[j] = grad.astype(jnp.bfloat16)
            return carry

        lax.fori_loop(0, count // UNROLL, body, 0)

    def piece_of(h, i):
        u, v, at_u, at_v = (x, z, at_x, at_z) if h == 0 else (z, x, at_z, at_x)
        split = pieces_of(per_owner)
        group = split[i]
        chunk = RING * group
        slot = h * (per_owner // 2) + sum(split[:i])
        first = slot * OWNERS
        uu, ud, uo = (u + 1) % RING, (u + 3) % RING, (u + 2) % RING
        return dict(
            n=h, v=v, to_uu=at_u(uu), to_ud=at_u(ud), vu=(v + 1) % RING, vd=(v + 3) % RING,
            vo=(v + 2) % RING, at_v=at_v, far=first + uo * chunk, next=first + uu * chunk,
            prev=first + ud * chunk, own=first + u * chunk, group=group, hc=chunk // 2, slot=slot,
            d=((e1, e2, e3, e4), (l1, l2, l3, l4))[i],
        )

    low, high = pl.ds(0, TILE // 2), pl.ds(TILE // 2, TILE // 2)

    def some(first, count):
        return buf.at[pl.ds(first, count)]

    def far_out(f):
        n, hc, d1 = f["n"], f["hc"], f["d"][0]
        tile_grads(f["far"], hc)
        f["far_u"] = send(some(f["far"], hc), d1.at[n, 0], f["to_uu"])
        tile_grads(f["far"] + hc, hc)
        f["far_d"] = send(some(f["far"] + hc, hc), d1.at[n, 1], f["to_ud"])

    def near_tiles(f):
        tile_grads(f["next"], 2 * f["hc"])
        tile_grads(f["prev"], 2 * f["hc"])

    def near_out(f):
        n, hc, d2 = f["n"], f["hc"], f["d"][1]
        f["near_u"] = send(some(f["next"] + hc, hc), d2.at[n, 0, pl.ds(hc, hc)], f["to_uu"])
        f["near_d"] = send(some(f["prev"], hc), d2.at[n, 1, pl.ds(0, hc)], f["to_ud"])

    def add_far(f, dst, side):
        d1 = f["d"][0]

        def body(i, carry):
            total = buf[dst + i].astype(jnp.float32) + d1[f["n"], side, i].astype(jnp.float32)
            buf[dst + i] = total.astype(jnp.bfloat16)
            return carry

        lax.fori_loop(0, f["hc"], body, 0)

    def sums_out(f):
        n, hc, d2 = f["n"], f["hc"], f["d"][1]
        f["far_u"].wait_recv()
        add_far(f, f["next"], 0)
        f["sum_u"] = send(some(f["next"], hc), d2.at[n, 0, pl.ds(0, hc)], f["to_uu"])
        f["far_d"].wait_recv()
        add_far(f, f["prev"] + hc, 1)
        f["sum_d"] = send(some(f["prev"] + hc, hc), d2.at[n, 1, pl.ds(hc, hc)], f["to_ud"])

    def settle(f, pos):
        n, group, d2 = f["n"], f["group"], f["d"][1]
        lead = pos * group

        def body(i, carry):
            total = buf[f["own"] + lead + i].astype(jnp.float32)
            total = total + d2[n, 0, lead + i].astype(jnp.float32)
            total = total + d2[n, 1, lead + i].astype(jnp.float32)
            buf[f["own"] + lead + i] = total.astype(jnp.bfloat16)
            return carry

        lax.fori_loop(0, group, body, 0)
        return pl.ds(f["own"] + lead, group)

    def second_out(f):
        n, group, (_, _, d3, d4) = f["n"], f["group"], f["d"]
        to_vu, to_vd = f["at_v"](f["vu"]), f["at_v"](f["vd"])
        for name in ("near_u", "near_d", "sum_u", "sum_d"):
            f[name].wait_recv()
        far = settle(f, f["vo"])
        f["far_u2"] = send(buf.at[far, low], d3.at[n, 0], to_vu)
        f["far_d2"] = send(buf.at[far, high], d3.at[n, 1], to_vd)
        following = settle(f, f["vu"])
        f["near_u2"] = send(buf.at[following, high], d4.at[n, 0, :, high], to_vu)
        preceding = settle(f, f["vd"])
        f["near_d2"] = send(buf.at[preceding, low], d4.at[n, 1, :, low], to_vd)
        settle(f, f["v"])

    def second_sums(f):
        n, group, (_, _, d3, d4) = f["n"], f["group"], f["d"]
        to_vu, to_vd = f["at_v"](f["vu"]), f["at_v"](f["vd"])
        for name, side, pos, half, dev in (("u", 0, "vu", low, to_vu), ("d", 1, "vd", high, to_vd)):
            f[f"far_{name}2"].wait_recv()
            dst = f["own"] + f[pos] * group

            def body(i, carry, dst=dst, half=half, side=side):
                total = buf[dst + i, half].astype(jnp.float32) + d3[n, side, i].astype(jnp.float32)
                buf[dst + i, half] = total.astype(jnp.bfloat16)
                return carry

            lax.fori_loop(0, group, body, 0)
            f[f"sum_{name}2"] = send(buf.at[pl.ds(dst, group), half], d4.at[n, side, :, half], dev)

    def finish(f):
        n, group, d4 = f["n"], f["group"], f["d"][3]
        for name in ("near_u2", "near_d2", "sum_u2", "sum_d2"):
            f[name].wait_recv()

        def body(i, carry):
            total = buf[f["own"] + f["v"] * group + i].astype(jnp.float32)
            total = total + d4[n, 0, i].astype(jnp.float32) + d4[n, 1, i].astype(jnp.float32)
            dw_ref[f["slot"] + i] = total.T
            return carry

        lax.fori_loop(0, group, body, 0)

    def add_rows(row, first, term):
        def body(i, carry):
            at = pl.ds(pl.multiple_of(i * row_step, row_step), row_step)
            to = pl.ds(pl.multiple_of(first + i * row_step, row_step), row_step)
            total = part[q, row, to].astype(jnp.float32) + yr1[term, at].astype(jnp.float32)
            part[q, row, to] = total.astype(jnp.bfloat16)
            return carry

        lax.fori_loop(0, hrows // row_step, body, 0)

    early = [piece_of(0, 0), piece_of(1, 0)]
    late = [piece_of(0, 1), piece_of(1, 1)]
    for f in early + late:
        far_out(f)
    for f in early:
        near_tiles(f)
    for f in early:
        sums_out(f)
    for f in early:
        near_out(f)
    for f in late:
        near_tiles(f)
    for f in early + late:
        tile_grads(f["own"], 2 * f["hc"])

    gi_up_far.wait_recv()
    add_rows(yu, 0, 0)
    gi_up_sum = send(part.at[q, yu, top], yr2.at[0, top], up)
    gi_down_far.wait_recv()
    add_rows(yd, hrows, 1)
    gi_down_sum = send(part.at[q, yd, bottom], yr2.at[1, bottom], down)

    for f in early:
        sent(f["sum_u"])
        sent(f["sum_d"])
    for f in late:
        sums_out(f)
    for f in early:
        sent(f["near_u"])
        sent(f["near_d"])
    for f in late:
        near_out(f)
    for f in early:
        second_out(f)
    for f in early:
        second_sums(f)
    for f in late:
        second_out(f)
    for copy in (gi_up_near, gi_down_near, gi_up_sum, gi_down_sum):
        copy.wait_recv()
    for f in late:
        second_sums(f)

    def finish_rows(i, carry):
        at = pl.ds(pl.multiple_of(i * row_step, row_step), row_step)
        total = part[q, y, at].astype(jnp.float32) + yr2[0, at].astype(jnp.float32)
        gi_ref[at, :] = (total + yr2[1, at].astype(jnp.float32)).astype(jnp.bfloat16)
        return carry

    lax.fori_loop(0, steps, finish_rows, 0)
    for f in early + late:
        finish(f)
    for copy in started:
        if all(copy is not gone for gone in left):
            copy.wait_send()


def per_device(x_seq, grad_out, w_tiles, block_rows, block_cols, counts, owner):
    rows, width = x_seq.shape
    tokens, shard_width = grad_out.shape
    slots = w_tiles.shape[0]
    col_blocks = shard_width // TILE
    per_owner = slots // OWNERS
    split = pieces_of(per_owner)
    lut_rows = pl.cdiv(pl.cdiv(slots, TILE) + pl.cdiv(width // TILE * col_blocks, TILE), 8) * 8

    bf16 = jnp.bfloat16
    any_space = pl.BlockSpec(memory_space=pl.ANY)
    smem = pl.BlockSpec(memory_space=pltpu.SMEM)
    vmem = pl.BlockSpec(memory_space=pltpu.VMEM)
    grad_in, owned = pl.pallas_call(
        kernel,
        out_shape=(
            pltpu.VMEM((rows, width), bf16),
            pltpu.VMEM((per_owner, TILE, TILE), jnp.float32),
        ),
        in_specs=[vmem, vmem, vmem, smem, any_space, any_space, any_space],
        out_specs=(vmem, vmem),
        scratch_shapes=[
            pltpu.VMEM((2 * RING, rows, width), bf16),
            pltpu.VMEM((2, RING, rows, width), bf16),
            pltpu.VMEM((RING, rows, width), bf16),
            pltpu.VMEM((tokens, shard_width), bf16),
            pltpu.VMEM((col_blocks + 1, TILE, tokens), bf16),
            pltpu.VMEM((slots + 1, TILE, TILE), bf16),
            pltpu.VMEM((2, rows // 2, width), bf16),
            pltpu.VMEM((2, rows, width), bf16),
            *[
                pltpu.VMEM((2, 2, *shape, TILE), bf16)
                for n in split
                for shape in ((2 * n, TILE), (4 * n, TILE), (n, TILE // 2), (n, TILE))
            ],
            pltpu.VMEM((lut_rows, TILE), jnp.int32),
            pltpu.SMEM((lut_rows, TILE), jnp.int32),
            pltpu.SemaphoreType.DMA((4,)),
            pltpu.SemaphoreType.DMA((NCOPY,)),
            pltpu.SemaphoreType.DMA((NCOPY,)),
        ],
        compiler_params=pltpu.CompilerParams(
            collective_id=0, has_side_effects=True, vmem_limit_bytes=60 * 1024 * 1024
        ),
        cost_estimate=pl.CostEstimate(
            flops=2 * tokens * shard_width * width + 2 * slots * tokens * TILE * TILE,
            bytes_accessed=2 * (slots * TILE * TILE + tokens * shard_width + 2 * rows * width)
            + 4 * per_owner * TILE * TILE,
            transcendentals=0,
        ),
    )(block_rows, block_cols, owner, counts, x_seq, grad_out, w_tiles)
    return grad_in, owned.reshape(1, per_owner, TILE, TILE)


def solution(mesh):
    return jax.shard_map(
        per_device,
        mesh=mesh,
        in_specs=(
            P(("dp", "tensor"), None),
            P("dp", "tensor"),
            P("tensor", None, None),
            P("tensor", None),
            P("tensor", None),
            P("tensor"),
            P("tensor", None),
        ),
        out_specs=(P(("dp", "tensor"), None), P("tensor", "dp", None, None)),
        check_vma=False,
    )
```

```python
import jax
import jax.numpy as jnp
from jax import lax
from jax.experimental import pallas as pl
from jax.experimental.pallas import tpu as pltpu
from jax.sharding import PartitionSpec as P

MESH = pl.DeviceIdType.MESH
RING = 4
TILE = 128
OWNERS = RING * RING
NCOPY = 80
COL_CHUNKS = 4
COL_STEP = 256
UNROLLS = (8, 4, 2, 1)


def pieces_of(per_owner):
    half = per_owner // 2
    late = half * 2 // 5
    return (half - late, late)


def fill_tables(rows_ref, cols_ref, owner_ref, counts, lut_v, col_blocks, blocks):
    slots = owner_ref.shape[1]
    per_owner = slots // OWNERS
    half = per_owner // 2
    early, late = pieces_of(per_owner)
    slot = lax.broadcasted_iota(jnp.int32, (1, slots), 1)
    live = (slot < counts[0]).astype(jnp.int32)

    def quotient(a, n, limit):
        return sum((a >= n * m).astype(jnp.int32) for m in range(1, limit))

    at = owner_ref[...]
    chip = quotient(at, per_owner, OWNERS)
    at = at - chip * per_owner
    x = quotient(chip, RING, RING)
    z = chip - x * RING
    h = (at >= half).astype(jnp.int32)
    at = at - h * half
    i = (at >= early).astype(jnp.int32)
    at = at - i * early
    u, v = x + h * (z - x), z + h * (x - z)
    place = (h * half + i * early) * OWNERS + (u * RING + v) * (early + i * (late - early)) + at
    code = rows_ref[...] * 16 + col_blocks + live * (cols_ref[...] - col_blocks)
    key = live * (rows_ref[...] * col_blocks + cols_ref[...] + 1) - 1

    places, tables = pl.cdiv(slots, TILE), pl.cdiv(blocks, TILE)
    totals = [jnp.zeros((1, TILE), jnp.int32) for _ in range(places + tables)]
    for first in range(0, slots, TILE):
        n = min(TILE, slots - first)

        def upright(a, first=first, n=n):
            return jnp.broadcast_to(a[:, first : first + n], (TILE, n)).T

        lane = lax.broadcasted_iota(jnp.int32, (n, TILE), 1)
        index = lax.broadcasted_iota(jnp.int32, (n, TILE), 0) + (first - slots)
        place_n, code_n, key_n = upright(place), upright(code), upright(key)
        for m in range(places + tables):
            wanted, had, value = (
                (lane + m * TILE, place_n, code_n) if m < places else (lane + (m - places) * TILE, key_n, index)
            )
            match = (had == wanted).astype(jnp.int32)
            if m < places:
                totals[m] = jnp.maximum(totals[m], jnp.max(match * value, axis=0, keepdims=True))
            else:
                totals[m] = jnp.minimum(totals[m], jnp.min(match * value, axis=0, keepdims=True))
    lut_v[...] = jnp.zeros_like(lut_v)
    for m, total in enumerate(totals):
        lut_v[m : m + 1, :] = total


def kernel(
    rows_ref, cols_ref, owner_ref, counts, x_ref, g_hbm, w_hbm, gi_ref, dw_ref,
    xg, part, pr, g, gt, buf, yr1, yr2, e1, e2, e3, e4, l1, l2, l3, l4, lut_v, lut_s, lsem, ssem, rsem,
):
    rows, width = x_ref.shape
    tokens, shard_width = g_hbm.shape
    slots = w_hbm.shape[0]
    col_blocks = shard_width // TILE
    per_owner = slots // OWNERS
    hrows = rows // 2
    top, bottom = pl.ds(0, hrows), pl.ds(hrows, hrows)
    quarters = [pl.ds(i * (rows // 4), rows // 4) for i in range(4)]

    p = lax.axis_index("dp")
    s = lax.axis_index("tensor")
    x, z = p // RING, p % RING
    y, q = s // 2, s % 2
    yu, yd, yo = (y + 1) % RING, (y + 3) % RING, (y + 2) % RING
    other = 1 - q

    def at_y(row, core):
        return (p, row * 2 + core)

    def at_x(pos):
        return (pos * RING + z, s)

    def at_z(pos):
        return (x * RING + pos, s)

    started = []

    def send(src, dst, device):
        i = len(started)
        copy = pltpu.make_async_remote_copy(
            src_ref=src, dst_ref=dst, send_sem=ssem.at[i], recv_sem=rsem.at[i],
            device_id=device, device_id_type=MESH,
        )
        copy.start()
        started.append(copy)
        return copy

    left = []

    def sent(copy):
        copy.wait_send()
        left.append(copy)

    up, down, across = at_y(yu, q), at_y(yd, q), at_y(y, other)

    load_x = pltpu.make_async_copy(x_ref, xg.at[s], lsem.at[0])
    load_g = pltpu.make_async_copy(g_hbm, g, lsem.at[1])
    load_w = pltpu.make_async_copy(w_hbm, buf.at[pl.ds(0, slots)], lsem.at[2])
    load_x.start()

    barrier = pltpu.get_barrier_semaphore()
    peers = [
        up, down, across,
        at_x((x + 1) % RING), at_x((x + 3) % RING), at_z((z + 1) % RING), at_z((z + 3) % RING),
    ]
    for peer in peers:
        pl.semaphore_signal(barrier, inc=1, device_id=peer, device_id_type=MESH)
    load_x.wait()
    pl.semaphore_wait(barrier, len(peers))

    up_top = send(xg.at[s, top], xg.at[s, top], up)
    down_bottom = send(xg.at[s, bottom], xg.at[s, bottom], down)
    up_bottom = send(xg.at[s, bottom], xg.at[s, bottom], up)
    down_top = send(xg.at[s, top], xg.at[s, top], down)
    sib_own = send(xg.at[s], xg.at[s], across)

    load_g.start()
    load_w.start()
    fill_tables(rows_ref, cols_ref, owner_ref, counts, lut_v, col_blocks, width // TILE * col_blocks)
    load_lut = pltpu.make_async_copy(lut_v, lut_s, lsem.at[3])
    load_lut.start()
    load_g.wait()
    for c in range(col_blocks):
        gt[c] = g[:, c * TILE : (c + 1) * TILE].T
    gt[col_blocks] = jnp.zeros((TILE, tokens), gt.dtype)
    buf[slots] = jnp.zeros((TILE, TILE), buf.dtype)
    load_w.wait()
    load_lut.wait()

    table_at = pl.cdiv(slots, TILE) * TILE

    def lut(i):
        return lut_s[lax.div(i, TILE), lax.rem(i, TILE)]

    cols_per_chunk = width // COL_CHUNKS
    blocks = COL_STEP // TILE

    def part_chunk(n):
        def body(i, carry):
            first = n * cols_per_chunk + i * COL_STEP
            first_block = n * (cols_per_chunk // TILE) + i * blocks
            weight = jnp.concatenate(
                [
                    jnp.concatenate(
                        [buf[lut(table_at + (first_block + b) * col_blocks + c) + slots] for c in range(col_blocks)], axis=1
                    )
                    for b in range(blocks)
                ],
                axis=0,
            )
            product = lax.dot_general(
                g[...], weight, (((1,), (1,)), ((), ())), preferred_element_type=jnp.float32
            )
            product = product.astype(jnp.bfloat16).reshape(RING, 2, rows, COL_STEP)
            columns = pl.ds(pl.multiple_of(first, COL_STEP), COL_STEP)
            for core in range(2):
                part[core, :, :, columns] = product[:, core]
            return carry

        lax.fori_loop(0, cols_per_chunk // COL_STEP, body, 0)
        columns = pl.ds(n * cols_per_chunk, cols_per_chunk)
        return send(part.at[other, :, :, columns], pr.at[:, :, columns], across)

    pair = [part_chunk(0), part_chunk(1)]
    up_top.wait_recv()
    from_down, from_up, from_far = yd * 2 + q, yu * 2 + q, yo * 2 + q
    fwd_up = [send(xg.at[from_down, at], xg.at[from_down, at], up) for at in quarters[:2]]
    down_bottom.wait_recv()
    fwd_down = [send(xg.at[from_up, at], xg.at[from_up, at], down) for at in quarters[2:]]
    pair += [part_chunk(2), part_chunk(3)]
    up_bottom.wait_recv()
    sib_down = send(xg.at[from_down], xg.at[from_down], across)
    down_top.wait_recv()
    sib_up = send(xg.at[from_up], xg.at[from_up], across)

    for copy in pair:
        copy.wait_recv()
    row_step = 16
    steps = rows // row_step

    def add_pair(i, carry):
        at = pl.ds(pl.multiple_of((i % steps) * row_step, row_step), row_step)
        row = i // steps
        total = part[q, row, at].astype(jnp.float32) + pr[row, at].astype(jnp.float32)
        part[q, row, at] = total.astype(jnp.bfloat16)
        return carry

    lax.fori_loop(0, RING * steps, add_pair, 0)

    sib_far = []
    for i in range(2):
        for copy, at in ((fwd_up[i], quarters[i]), (fwd_down[i], quarters[i + 2])):
            copy.wait_recv()
            sib_far.append(send(xg.at[from_far, at], xg.at[from_far, at], across))

    gi_up_far = send(part.at[q, yo, top], yr1.at[0], up)
    gi_down_far = send(part.at[q, yo, bottom], yr1.at[1], down)
    gi_up_near = send(part.at[q, yu, bottom], yr2.at[0, bottom], up)
    gi_down_near = send(part.at[q, yd, top], yr2.at[1, top], down)

    for copy in (sib_own, sib_down, sib_up, *sib_far):
        copy.wait_recv()

    def tile_grads(first, count):
        unroll = next(n for n in UNROLLS if count % n == 0)

        def body(i, carry):
            for k in range(unroll):
                j = first + i * unroll + k
                code = lut(j)
                rhs = xg[:, :, pl.ds(lax.div(code, 16) * TILE, TILE)].reshape(tokens, TILE)
                grad = jnp.dot(gt[lax.rem(code, 16)], rhs, preferred_element_type=jnp.float32)
                buf[j] = grad.astype(jnp.bfloat16)
            return carry

        lax.fori_loop(0, count // unroll, body, 0)

    def piece_of(h, i):
        u, v, at_u, at_v = (x, z, at_x, at_z) if h == 0 else (z, x, at_z, at_x)
        split = pieces_of(per_owner)
        group = split[i]
        chunk = RING * group
        slot = h * (per_owner // 2) + sum(split[:i])
        first = slot * OWNERS
        uu, ud, uo = (u + 1) % RING, (u + 3) % RING, (u + 2) % RING
        return dict(
            n=h, v=v, to_uu=at_u(uu), to_ud=at_u(ud), vu=(v + 1) % RING, vd=(v + 3) % RING,
            vo=(v + 2) % RING, at_v=at_v, far=first + uo * chunk, next=first + uu * chunk,
            prev=first + ud * chunk, own=first + u * chunk, group=group, hc=chunk // 2, slot=slot,
            d=((e1, e2, e3, e4), (l1, l2, l3, l4))[i], out=([], []),
        )

    low, high = pl.ds(0, TILE // 2), pl.ds(TILE // 2, TILE // 2)

    def some(first, count):
        return buf.at[pl.ds(first, count)]

    def far_out(pieces, first, count):
        for f in pieces:
            n, hc, d1 = f["n"], f["hc"], f["d"][0]
            for side, to in enumerate((f["to_uu"], f["to_ud"])):
                at = f["far"] + side * hc + first
                tile_grads(at, count)
                f["out"][side].append(send(some(at, count), d1.at[n, side, pl.ds(first, count)], to))

    def near_tiles(f):
        tile_grads(f["next"], 2 * f["hc"])
        tile_grads(f["prev"], 2 * f["hc"])

    def near_out(f):
        n, hc, d2 = f["n"], f["hc"], f["d"][1]
        f["near_u"] = send(some(f["next"] + hc, hc), d2.at[n, 0, pl.ds(hc, hc)], f["to_uu"])
        f["near_d"] = send(some(f["prev"], hc), d2.at[n, 1, pl.ds(0, hc)], f["to_ud"])

    def add_far(f, dst, side):
        d1 = f["d"][0]

        def body(i, carry):
            total = buf[dst + i].astype(jnp.float32) + d1[f["n"], side, i].astype(jnp.float32)
            buf[dst + i] = total.astype(jnp.bfloat16)
            return carry

        lax.fori_loop(0, f["hc"], body, 0)

    def sums_out(f):
        n, hc, d2 = f["n"], f["hc"], f["d"][1]
        for copy in f["out"][0]:
            copy.wait_recv()
        add_far(f, f["next"], 0)
        f["sum_u"] = send(some(f["next"], hc), d2.at[n, 0, pl.ds(0, hc)], f["to_uu"])
        for copy in f["out"][1]:
            copy.wait_recv()
        add_far(f, f["prev"] + hc, 1)
        f["sum_d"] = send(some(f["prev"] + hc, hc), d2.at[n, 1, pl.ds(hc, hc)], f["to_ud"])

    def settle(f, pos):
        n, group, d2 = f["n"], f["group"], f["d"][1]
        lead = pos * group

        def body(i, carry):
            total = buf[f["own"] + lead + i].astype(jnp.float32)
            total = total + d2[n, 0, lead + i].astype(jnp.float32)
            total = total + d2[n, 1, lead + i].astype(jnp.float32)
            buf[f["own"] + lead + i] = total.astype(jnp.bfloat16)
            return carry

        lax.fori_loop(0, group, body, 0)
        return pl.ds(f["own"] + lead, group)

    def second_out(f):
        n, group, (_, _, d3, d4) = f["n"], f["group"], f["d"]
        to_vu, to_vd = f["at_v"](f["vu"]), f["at_v"](f["vd"])
        for name in ("near_u", "near_d", "sum_u", "sum_d"):
            f[name].wait_recv()
        far = settle(f, f["vo"])
        f["far_u2"] = send(buf.at[far, low], d3.at[n, 0], to_vu)
        f["far_d2"] = send(buf.at[far, high], d3.at[n, 1], to_vd)
        following = settle(f, f["vu"])
        f["near_u2"] = send(buf.at[following, high], d4.at[n, 0, :, high], to_vu)
        preceding = settle(f, f["vd"])
        f["near_d2"] = send(buf.at[preceding, low], d4.at[n, 1, :, low], to_vd)
        settle(f, f["v"])

    def second_sums(f):
        n, group, (_, _, d3, d4) = f["n"], f["group"], f["d"]
        to_vu, to_vd = f["at_v"](f["vu"]), f["at_v"](f["vd"])
        for name, side, pos, half, dev in (("u", 0, "vu", low, to_vu), ("d", 1, "vd", high, to_vd)):
            f[f"far_{name}2"].wait_recv()
            dst = f["own"] + f[pos] * group

            def body(i, carry, dst=dst, half=half, side=side):
                total = buf[dst + i, half].astype(jnp.float32) + d3[n, side, i].astype(jnp.float32)
                buf[dst + i, half] = total.astype(jnp.bfloat16)
                return carry

            lax.fori_loop(0, group, body, 0)
            f[f"sum_{name}2"] = send(buf.at[pl.ds(dst, group), half], d4.at[n, side, :, half], dev)

    def finish(f):
        n, group, d4 = f["n"], f["group"], f["d"][3]
        for name in ("near_u2", "near_d2", "sum_u2", "sum_d2"):
            f[name].wait_recv()

        def body(i, carry):
            total = buf[f["own"] + f["v"] * group + i].astype(jnp.float32)
            total = total + d4[n, 0, i].astype(jnp.float32) + d4[n, 1, i].astype(jnp.float32)
            dw_ref[f["slot"] + i] = total.T
            return carry

        lax.fori_loop(0, group, body, 0)

    def add_rows(row, first, term):
        def body(i, carry):
            at = pl.ds(pl.multiple_of(i * row_step, row_step), row_step)
            to = pl.ds(pl.multiple_of(first + i * row_step, row_step), row_step)
            total = part[q, row, to].astype(jnp.float32) + yr1[term, at].astype(jnp.float32)
            part[q, row, to] = total.astype(jnp.bfloat16)
            return carry

        lax.fori_loop(0, hrows // row_step, body, 0)

    early = [piece_of(0, 0), piece_of(1, 0)]
    late = [piece_of(0, 1), piece_of(1, 1)]
    lead = 4
    far_out(early, 0, lead)
    far_out(early, lead, early[0]["hc"] - lead)
    far_out(late, 0, late[0]["hc"])
    for f in early:
        near_tiles(f)
    for f in early:
        sums_out(f)
    for f in early:
        near_out(f)
    for f in late:
        near_tiles(f)
    for f in early + late:
        tile_grads(f["own"], 2 * f["hc"])

    gi_up_far.wait_recv()
    add_rows(yu, 0, 0)
    gi_up_sum = send(part.at[q, yu, top], yr2.at[0, top], up)
    gi_down_far.wait_recv()
    add_rows(yd, hrows, 1)
    gi_down_sum = send(part.at[q, yd, bottom], yr2.at[1, bottom], down)

    for f in early:
        sent(f["sum_u"])
        sent(f["sum_d"])
    for f in late:
        sums_out(f)
    for f in early:
        sent(f["near_u"])
        sent(f["near_d"])
    for f in late:
        near_out(f)
    for f in early:
        second_out(f)
    for f in early:
        second_sums(f)
    for f in late:
        second_out(f)
    for copy in (gi_up_near, gi_down_near, gi_up_sum, gi_down_sum):
        copy.wait_recv()
    for f in late:
        second_sums(f)

    def finish_rows(i, carry):
        at = pl.ds(pl.multiple_of(i * row_step, row_step), row_step)
        total = part[q, y, at].astype(jnp.float32) + yr2[0, at].astype(jnp.float32)
        gi_ref[at, :] = (total + yr2[1, at].astype(jnp.float32)).astype(jnp.bfloat16)
        return carry

    lax.fori_loop(0, steps, finish_rows, 0)
    for f in early + late:
        finish(f)
    for copy in started:
        if all(copy is not gone for gone in left):
            copy.wait_send()


def per_device(x_seq, grad_out, w_tiles, block_rows, block_cols, counts, owner):
    rows, width = x_seq.shape
    tokens, shard_width = grad_out.shape
    slots = w_tiles.shape[0]
    col_blocks = shard_width // TILE
    per_owner = slots // OWNERS
    split = pieces_of(per_owner)
    lut_rows = pl.cdiv(pl.cdiv(slots, TILE) + pl.cdiv(width // TILE * col_blocks, TILE), 8) * 8

    bf16 = jnp.bfloat16
    any_space = pl.BlockSpec(memory_space=pl.ANY)
    smem = pl.BlockSpec(memory_space=pltpu.SMEM)
    vmem = pl.BlockSpec(memory_space=pltpu.VMEM)
    grad_in, owned = pl.pallas_call(
        kernel,
        out_shape=(
            pltpu.VMEM((rows, width), bf16),
            pltpu.VMEM((per_owner, TILE, TILE), jnp.float32),
        ),
        in_specs=[vmem, vmem, vmem, smem, any_space, any_space, any_space],
        out_specs=(vmem, vmem),
        scratch_shapes=[
            pltpu.VMEM((2 * RING, rows, width), bf16),
            pltpu.VMEM((2, RING, rows, width), bf16),
            pltpu.VMEM((RING, rows, width), bf16),
            pltpu.VMEM((tokens, shard_width), bf16),
            pltpu.VMEM((col_blocks + 1, TILE, tokens), bf16),
            pltpu.VMEM((slots + 1, TILE, TILE), bf16),
            pltpu.VMEM((2, rows // 2, width), bf16),
            pltpu.VMEM((2, rows, width), bf16),
            *[
                pltpu.VMEM((2, 2, *shape, TILE), bf16)
                for n in split
                for shape in ((2 * n, TILE), (4 * n, TILE), (n, TILE // 2), (n, TILE))
            ],
            pltpu.VMEM((lut_rows, TILE), jnp.int32),
            pltpu.SMEM((lut_rows, TILE), jnp.int32),
            pltpu.SemaphoreType.DMA((4,)),
            pltpu.SemaphoreType.DMA((NCOPY,)),
            pltpu.SemaphoreType.DMA((NCOPY,)),
        ],
        compiler_params=pltpu.CompilerParams(
            collective_id=0, has_side_effects=True, vmem_limit_bytes=60 * 1024 * 1024
        ),
        cost_estimate=pl.CostEstimate(
            flops=2 * tokens * shard_width * width + 2 * slots * tokens * TILE * TILE,
            bytes_accessed=2 * (slots * TILE * TILE + tokens * shard_width + 2 * rows * width)
            + 4 * per_owner * TILE * TILE,
            transcendentals=0,
        ),
    )(block_rows, block_cols, owner, counts, x_seq, grad_out, w_tiles)
    return grad_in, owned.reshape(1, per_owner, TILE, TILE)


def solution(mesh):
    return jax.shard_map(
        per_device,
        mesh=mesh,
        in_specs=(
            P(("dp", "tensor"), None),
            P("dp", "tensor"),
            P("tensor", None, None),
            P("tensor", None),
            P("tensor", None),
            P("tensor"),
            P("tensor", None),
        ),
        out_specs=(P(("dp", "tensor"), None), P("tensor", "dp", None, None)),
        check_vma=False,
    )
```

```python
import jax
import jax.numpy as jnp
from jax import lax
from jax.experimental import pallas as pl
from jax.experimental.pallas import tpu as pltpu
from jax.sharding import PartitionSpec as P

MESH = pl.DeviceIdType.MESH
RING = 4
TILE = 128
OWNERS = RING * RING
NCOPY = 80
COL_CHUNKS = 4
COL_STEP = 256
UNROLLS = (8, 4, 2, 1)


def pieces_of(per_owner):
    half = per_owner // 2
    late = half * 2 // 5
    return (half - late, late)


def fill_tables(rows_ref, cols_ref, owner_ref, counts, lut_v, col_blocks, blocks):
    slots = owner_ref.shape[1]
    per_owner = slots // OWNERS
    half = per_owner // 2
    early, late = pieces_of(per_owner)
    slot = lax.broadcasted_iota(jnp.int32, (1, slots), 1)
    live = (slot < counts[0]).astype(jnp.int32)

    def quotient(a, n, limit):
        return sum((a >= n * m).astype(jnp.int32) for m in range(1, limit))

    at = owner_ref[...]
    chip = quotient(at, per_owner, OWNERS)
    at = at - chip * per_owner
    x = quotient(chip, RING, RING)
    z = chip - x * RING
    h = (at >= half).astype(jnp.int32)
    at = at - h * half
    i = (at >= early).astype(jnp.int32)
    at = at - i * early
    u, v = x + h * (z - x), z + h * (x - z)
    place = (h * half + i * early) * OWNERS + (u * RING + v) * (early + i * (late - early)) + at
    code = rows_ref[...] * 16 + col_blocks + live * (cols_ref[...] - col_blocks)
    key = live * (rows_ref[...] * col_blocks + cols_ref[...] + 1) - 1

    places, tables = pl.cdiv(slots, TILE), pl.cdiv(blocks, TILE)
    totals = [jnp.zeros((1, TILE), jnp.int32) for _ in range(places + tables)]
    for first in range(0, slots, TILE):
        n = min(TILE, slots - first)

        def upright(a, first=first, n=n):
            return jnp.broadcast_to(a[:, first : first + n], (TILE, n)).T

        lane = lax.broadcasted_iota(jnp.int32, (n, TILE), 1)
        index = lax.broadcasted_iota(jnp.int32, (n, TILE), 0) + (first - slots)
        place_n, code_n, key_n = upright(place), upright(code), upright(key)
        for m in range(places + tables):
            wanted, had, value = (
                (lane + m * TILE, place_n, code_n) if m < places else (lane + (m - places) * TILE, key_n, index)
            )
            match = (had == wanted).astype(jnp.int32)
            if m < places:
                totals[m] = jnp.maximum(totals[m], jnp.max(match * value, axis=0, keepdims=True))
            else:
                totals[m] = jnp.minimum(totals[m], jnp.min(match * value, axis=0, keepdims=True))
    lut_v[...] = jnp.zeros_like(lut_v)
    for m, total in enumerate(totals):
        lut_v[m : m + 1, :] = total


def copy_out(gi_in, dw_in, gi_out, dw_out, sem):
    copies = [pltpu.make_async_copy(gi_in, gi_out, sem.at[0]), pltpu.make_async_copy(dw_in, dw_out, sem.at[1])]
    for copy in copies:
        copy.start()
    for copy in copies:
        copy.wait()


def kernel(
    rows_ref, cols_ref, owner_ref, counts, x_ref, g_hbm, w_hbm, gi_ref, dw_ref,
    xg, part, pr, g, gt, buf, yr1, yr2, e1, e2, e3, e4, l1, l2, l3, l4, lut_v, lut_s, lsem, ssem, rsem,
):
    rows, width = x_ref.shape
    tokens, shard_width = g_hbm.shape
    slots = w_hbm.shape[0]
    col_blocks = shard_width // TILE
    per_owner = slots // OWNERS
    hrows = rows // 2
    top, bottom = pl.ds(0, hrows), pl.ds(hrows, hrows)
    quarters = [pl.ds(i * (rows // 4), rows // 4) for i in range(4)]

    p = lax.axis_index("dp")
    s = lax.axis_index("tensor")
    x, z = p // RING, p % RING
    y, q = s // 2, s % 2
    yu, yd, yo = (y + 1) % RING, (y + 3) % RING, (y + 2) % RING
    other = 1 - q

    def at_y(row, core):
        return (p, row * 2 + core)

    def at_x(pos):
        return (pos * RING + z, s)

    def at_z(pos):
        return (x * RING + pos, s)

    started = []

    def send(src, dst, device):
        i = len(started)
        copy = pltpu.make_async_remote_copy(
            src_ref=src, dst_ref=dst, send_sem=ssem.at[i], recv_sem=rsem.at[i],
            device_id=device, device_id_type=MESH,
        )
        copy.start()
        started.append(copy)
        return copy

    left = []

    def sent(copy):
        copy.wait_send()
        left.append(copy)

    up, down, across = at_y(yu, q), at_y(yd, q), at_y(y, other)

    load_x = pltpu.make_async_copy(x_ref, xg.at[s], lsem.at[0])
    load_g = pltpu.make_async_copy(g_hbm, g, lsem.at[1])
    load_w = pltpu.make_async_copy(w_hbm, buf.at[pl.ds(0, slots)], lsem.at[2])
    load_x.start()

    barrier = pltpu.get_barrier_semaphore()
    peers = [
        up, down, across,
        at_x((x + 1) % RING), at_x((x + 3) % RING), at_z((z + 1) % RING), at_z((z + 3) % RING),
    ]
    for peer in peers:
        pl.semaphore_signal(barrier, inc=1, device_id=peer, device_id_type=MESH)
    pl.semaphore_wait(barrier, len(peers))

    up_top = send(x_ref.at[top], xg.at[s, top], up)
    down_bottom = send(x_ref.at[bottom], xg.at[s, bottom], down)
    up_bottom = send(x_ref.at[bottom], xg.at[s, bottom], up)
    down_top = send(x_ref.at[top], xg.at[s, top], down)
    load_x.wait()
    sib_own = send(xg.at[s], xg.at[s], across)

    load_g.start()
    load_w.start()
    fill_tables(rows_ref, cols_ref, owner_ref, counts, lut_v, col_blocks, width // TILE * col_blocks)
    load_lut = pltpu.make_async_copy(lut_v, lut_s, lsem.at[3])
    load_lut.start()
    load_g.wait()
    for c in range(col_blocks):
        gt[c] = g[:, c * TILE : (c + 1) * TILE].T
    gt[col_blocks] = jnp.zeros((TILE, tokens), gt.dtype)
    buf[slots] = jnp.zeros((TILE, TILE), buf.dtype)
    load_w.wait()
    load_lut.wait()

    table_at = pl.cdiv(slots, TILE) * TILE

    def lut(i):
        return lut_s[lax.div(i, TILE), lax.rem(i, TILE)]

    cols_per_chunk = width // COL_CHUNKS
    blocks = COL_STEP // TILE

    def part_chunk(n):
        def body(i, carry):
            first = n * cols_per_chunk + i * COL_STEP
            first_block = n * (cols_per_chunk // TILE) + i * blocks
            weight = jnp.concatenate(
                [
                    jnp.concatenate(
                        [buf[lut(table_at + (first_block + b) * col_blocks + c) + slots] for c in range(col_blocks)], axis=1
                    )
                    for b in range(blocks)
                ],
                axis=0,
            )
            product = lax.dot_general(
                g[...], weight, (((1,), (1,)), ((), ())), preferred_element_type=jnp.float32
            )
            product = product.astype(jnp.bfloat16).reshape(RING, 2, rows, COL_STEP)
            columns = pl.ds(pl.multiple_of(first, COL_STEP), COL_STEP)
            for core in range(2):
                part[core, :, :, columns] = product[:, core]
            return carry

        lax.fori_loop(0, cols_per_chunk // COL_STEP, body, 0)
        columns = pl.ds(n * cols_per_chunk, cols_per_chunk)
        return send(part.at[other, :, :, columns], pr.at[:, :, columns], across)

    pair = [part_chunk(0), part_chunk(1)]
    up_top.wait_recv()
    from_down, from_up, from_far = yd * 2 + q, yu * 2 + q, yo * 2 + q
    fwd_up = [send(xg.at[from_down, at], xg.at[from_down, at], up) for at in quarters[:2]]
    down_bottom.wait_recv()
    fwd_down = [send(xg.at[from_up, at], xg.at[from_up, at], down) for at in quarters[2:]]
    pair += [part_chunk(2), part_chunk(3)]
    up_bottom.wait_recv()
    sib_down = send(xg.at[from_down], xg.at[from_down], across)
    down_top.wait_recv()
    sib_up = send(xg.at[from_up], xg.at[from_up], across)

    for copy in pair:
        copy.wait_recv()
    row_step = 16
    steps = rows // row_step

    def add_pair(i, carry):
        at = pl.ds(pl.multiple_of((i % steps) * row_step, row_step), row_step)
        row = i // steps
        total = part[q, row, at].astype(jnp.float32) + pr[row, at].astype(jnp.float32)
        part[q, row, at] = total.astype(jnp.bfloat16)
        return carry

    lax.fori_loop(0, RING * steps, add_pair, 0)

    sib_far = []
    for i in range(2):
        for copy, at in ((fwd_up[i], quarters[i]), (fwd_down[i], quarters[i + 2])):
            copy.wait_recv()
            sib_far.append(send(xg.at[from_far, at], xg.at[from_far, at], across))

    gi_up_far = send(part.at[q, yo, top], yr1.at[0], up)
    gi_down_far = send(part.at[q, yo, bottom], yr1.at[1], down)
    gi_up_near = send(part.at[q, yu, bottom], yr2.at[0, bottom], up)
    gi_down_near = send(part.at[q, yd, top], yr2.at[1, top], down)

    for copy in (sib_own, sib_down, sib_up, *sib_far):
        copy.wait_recv()

    def tile_grads(first, count):
        unroll = next(n for n in UNROLLS if count % n == 0)

        def body(i, carry):
            for k in range(unroll):
                j = first + i * unroll + k
                code = lut(j)
                rhs = xg[:, :, pl.ds(lax.div(code, 16) * TILE, TILE)].reshape(tokens, TILE)
                grad = jnp.dot(gt[lax.rem(code, 16)], rhs, preferred_element_type=jnp.float32)
                buf[j] = grad.astype(jnp.bfloat16)
            return carry

        lax.fori_loop(0, count // unroll, body, 0)

    def piece_of(h, i):
        u, v, at_u, at_v = (x, z, at_x, at_z) if h == 0 else (z, x, at_z, at_x)
        split = pieces_of(per_owner)
        group = split[i]
        chunk = RING * group
        slot = h * (per_owner // 2) + sum(split[:i])
        first = slot * OWNERS
        uu, ud, uo = (u + 1) % RING, (u + 3) % RING, (u + 2) % RING
        return dict(
            n=h, v=v, to_uu=at_u(uu), to_ud=at_u(ud), vu=(v + 1) % RING, vd=(v + 3) % RING,
            vo=(v + 2) % RING, at_v=at_v, far=first + uo * chunk, next=first + uu * chunk,
            prev=first + ud * chunk, own=first + u * chunk, group=group, hc=chunk // 2, slot=slot,
            d=((e1, e2, e3, e4), (l1, l2, l3, l4))[i], out=([], []),
        )

    low, high = pl.ds(0, TILE // 2), pl.ds(TILE // 2, TILE // 2)

    def some(first, count):
        return buf.at[pl.ds(first, count)]

    def far_out(pieces, first, count):
        for f in pieces:
            n, hc, d1 = f["n"], f["hc"], f["d"][0]
            for side, to in enumerate((f["to_uu"], f["to_ud"])):
                at = f["far"] + side * hc + first
                tile_grads(at, count)
                f["out"][side].append(send(some(at, count), d1.at[n, side, pl.ds(first, count)], to))

    def near_tiles(f):
        tile_grads(f["next"], 2 * f["hc"])
        tile_grads(f["prev"], 2 * f["hc"])

    def near_out(f):
        n, hc, d2 = f["n"], f["hc"], f["d"][1]
        f["near_u"] = send(some(f["next"] + hc, hc), d2.at[n, 0, pl.ds(hc, hc)], f["to_uu"])
        f["near_d"] = send(some(f["prev"], hc), d2.at[n, 1, pl.ds(0, hc)], f["to_ud"])

    def add_far(f, dst, side):
        d1 = f["d"][0]

        def body(i, carry):
            total = buf[dst + i].astype(jnp.float32) + d1[f["n"], side, i].astype(jnp.float32)
            buf[dst + i] = total.astype(jnp.bfloat16)
            return carry

        lax.fori_loop(0, f["hc"], body, 0)

    def sums_out(f):
        n, hc, d2 = f["n"], f["hc"], f["d"][1]
        for copy in f["out"][0]:
            copy.wait_recv()
        add_far(f, f["next"], 0)
        f["sum_u"] = send(some(f["next"], hc), d2.at[n, 0, pl.ds(0, hc)], f["to_uu"])
        for copy in f["out"][1]:
            copy.wait_recv()
        add_far(f, f["prev"] + hc, 1)
        f["sum_d"] = send(some(f["prev"] + hc, hc), d2.at[n, 1, pl.ds(hc, hc)], f["to_ud"])

    def settle(f, pos):
        n, group, d2 = f["n"], f["group"], f["d"][1]
        lead = pos * group

        def body(i, carry):
            total = buf[f["own"] + lead + i].astype(jnp.float32)
            total = total + d2[n, 0, lead + i].astype(jnp.float32)
            total = total + d2[n, 1, lead + i].astype(jnp.float32)
            buf[f["own"] + lead + i] = total.astype(jnp.bfloat16)
            return carry

        lax.fori_loop(0, group, body, 0)
        return pl.ds(f["own"] + lead, group)

    def second_out(f):
        n, group, (_, _, d3, d4) = f["n"], f["group"], f["d"]
        to_vu, to_vd = f["at_v"](f["vu"]), f["at_v"](f["vd"])
        for name in ("near_u", "near_d", "sum_u", "sum_d"):
            f[name].wait_recv()
        far = settle(f, f["vo"])
        f["far_u2"] = send(buf.at[far, low], d3.at[n, 0], to_vu)
        f["far_d2"] = send(buf.at[far, high], d3.at[n, 1], to_vd)
        following = settle(f, f["vu"])
        f["near_u2"] = send(buf.at[following, high], d4.at[n, 0, :, high], to_vu)
        preceding = settle(f, f["vd"])
        f["near_d2"] = send(buf.at[preceding, low], d4.at[n, 1, :, low], to_vd)
        settle(f, f["v"])

    def second_sums(f):
        n, group, (_, _, d3, d4) = f["n"], f["group"], f["d"]
        to_vu, to_vd = f["at_v"](f["vu"]), f["at_v"](f["vd"])
        for name, side, pos, half, dev in (("u", 0, "vu", low, to_vu), ("d", 1, "vd", high, to_vd)):
            f[f"far_{name}2"].wait_recv()
            dst = f["own"] + f[pos] * group

            def body(i, carry, dst=dst, half=half, side=side):
                total = buf[dst + i, half].astype(jnp.float32) + d3[n, side, i].astype(jnp.float32)
                buf[dst + i, half] = total.astype(jnp.bfloat16)
                return carry

            lax.fori_loop(0, group, body, 0)
            f[f"sum_{name}2"] = send(buf.at[pl.ds(dst, group), half], d4.at[n, side, :, half], dev)

    def finish(f):
        n, group, d4 = f["n"], f["group"], f["d"][3]
        for name in ("near_u2", "near_d2", "sum_u2", "sum_d2"):
            f[name].wait_recv()

        def body(i, carry):
            total = buf[f["own"] + f["v"] * group + i].astype(jnp.float32)
            total = total + d4[n, 0, i].astype(jnp.float32) + d4[n, 1, i].astype(jnp.float32)
            dw_ref[f["slot"] + i] = total.T
            return carry

        lax.fori_loop(0, group, body, 0)

    def add_rows(row, first, term):
        def body(i, carry):
            at = pl.ds(pl.multiple_of(i * row_step, row_step), row_step)
            to = pl.ds(pl.multiple_of(first + i * row_step, row_step), row_step)
            total = part[q, row, to].astype(jnp.float32) + yr1[term, at].astype(jnp.float32)
            part[q, row, to] = total.astype(jnp.bfloat16)
            return carry

        lax.fori_loop(0, hrows // row_step, body, 0)

    early = [piece_of(0, 0), piece_of(1, 0)]
    late = [piece_of(0, 1), piece_of(1, 1)]
    lead = 4
    far_out(early, 0, lead)
    far_out(early, lead, early[0]["hc"] - lead)
    far_out(late, 0, late[0]["hc"])
    for f in early:
        near_tiles(f)
    for f in early:
        sums_out(f)
    for f in early:
        near_out(f)
    for f in late:
        near_tiles(f)
    for f in early + late:
        tile_grads(f["own"], 2 * f["hc"])

    gi_up_far.wait_recv()
    add_rows(yu, 0, 0)
    gi_up_sum = send(part.at[q, yu, top], yr2.at[0, top], up)
    gi_down_far.wait_recv()
    add_rows(yd, hrows, 1)
    gi_down_sum = send(part.at[q, yd, bottom], yr2.at[1, bottom], down)

    for f in early:
        sent(f["sum_u"])
        sent(f["sum_d"])
    for f in late:
        sums_out(f)
    for f in early:
        sent(f["near_u"])
        sent(f["near_d"])
    for f in late:
        near_out(f)
    for f in early:
        second_out(f)
    for f in early:
        second_sums(f)
    for f in late:
        second_out(f)
    for copy in (gi_up_near, gi_down_near, gi_up_sum, gi_down_sum):
        copy.wait_recv()
    for f in late:
        second_sums(f)

    def finish_rows(i, carry):
        at = pl.ds(pl.multiple_of(i * row_step, row_step), row_step)
        total = part[q, y, at].astype(jnp.float32) + yr2[0, at].astype(jnp.float32)
        gi_ref[at, :] = (total + yr2[1, at].astype(jnp.float32)).astype(jnp.bfloat16)
        return carry

    lax.fori_loop(0, steps, finish_rows, 0)
    for f in early + late:
        finish(f)
    for copy in started:
        if all(copy is not gone for gone in left):
            copy.wait_send()


def per_device(x_seq, grad_out, w_tiles, block_rows, block_cols, counts, owner):
    rows, width = x_seq.shape
    tokens, shard_width = grad_out.shape
    slots = w_tiles.shape[0]
    col_blocks = shard_width // TILE
    per_owner = slots // OWNERS
    split = pieces_of(per_owner)
    lut_rows = pl.cdiv(pl.cdiv(slots, TILE) + pl.cdiv(width // TILE * col_blocks, TILE), 8) * 8

    bf16 = jnp.bfloat16
    any_space = pl.BlockSpec(memory_space=pl.ANY)
    smem = pl.BlockSpec(memory_space=pltpu.SMEM)
    vmem = pl.BlockSpec(memory_space=pltpu.VMEM)
    grad_in, owned = pl.pallas_call(
        kernel,
        out_shape=(
            pltpu.VMEM((rows, width), bf16),
            pltpu.VMEM((per_owner, TILE, TILE), jnp.float32),
        ),
        in_specs=[vmem, vmem, vmem, smem, any_space, any_space, any_space],
        out_specs=(vmem, vmem),
        scratch_shapes=[
            pltpu.VMEM((2 * RING, rows, width), bf16),
            pltpu.VMEM((2, RING, rows, width), bf16),
            pltpu.VMEM((RING, rows, width), bf16),
            pltpu.VMEM((tokens, shard_width), bf16),
            pltpu.VMEM((col_blocks + 1, TILE, tokens), bf16),
            pltpu.VMEM((slots + 1, TILE, TILE), bf16),
            pltpu.VMEM((2, rows // 2, width), bf16),
            pltpu.VMEM((2, rows, width), bf16),
            *[
                pltpu.VMEM((2, 2, *shape, TILE), bf16)
                for n in split
                for shape in ((2 * n, TILE), (4 * n, TILE), (n, TILE // 2), (n, TILE))
            ],
            pltpu.VMEM((lut_rows, TILE), jnp.int32),
            pltpu.SMEM((lut_rows, TILE), jnp.int32),
            pltpu.SemaphoreType.DMA((4,)),
            pltpu.SemaphoreType.DMA((NCOPY,)),
            pltpu.SemaphoreType.DMA((NCOPY,)),
        ],
        compiler_params=pltpu.CompilerParams(
            collective_id=0, has_side_effects=True, vmem_limit_bytes=60 * 1024 * 1024
        ),
        cost_estimate=pl.CostEstimate(
            flops=2 * tokens * shard_width * width + 2 * slots * tokens * TILE * TILE,
            bytes_accessed=2 * (slots * TILE * TILE + tokens * shard_width + 2 * rows * width)
            + 4 * per_owner * TILE * TILE,
            transcendentals=0,
        ),
    )(block_rows, block_cols, owner, counts, x_seq, grad_out, w_tiles)
    grad_in, owned = pl.pallas_call(
        copy_out,
        out_shape=(
            jax.ShapeDtypeStruct((rows, width), bf16),
            jax.ShapeDtypeStruct((per_owner, TILE, TILE), jnp.float32),
        ),
        in_specs=[vmem, vmem],
        out_specs=(any_space, any_space),
        scratch_shapes=[pltpu.SemaphoreType.DMA((2,))],
        compiler_params=pltpu.CompilerParams(vmem_limit_bytes=4 * 1024 * 1024),
    )(grad_in, owned)
    return grad_in, owned.reshape(1, per_owner, TILE, TILE)


def solution(mesh):
    return jax.shard_map(
        per_device,
        mesh=mesh,
        in_specs=(
            P(("dp", "tensor"), None),
            P("dp", "tensor"),
            P("tensor", None, None),
            P("tensor", None),
            P("tensor", None),
            P("tensor"),
            P("tensor", None),
        ),
        out_specs=(P(("dp", "tensor"), None), P("tensor", "dp", None, None)),
        check_vma=False,
    )
```
